256 devices in a mesh: xi: 4 (over x), eta: 2 (over core), zeta: 32 (over z, y).
Axes of the slice: x: 4, y: 4, z: 8, core: 2. Of those that a mesh axis runs over, the one named last changes fastest.
Arguments:
- state: float32 [5, 32, 64, 4096], P(None, 'xi', 'eta', 'zeta'), may hold values from -6 to 6
- radius: float32 [32, 64, 4096], P('xi', 'eta', 'zeta'), may hold values from 0.5 to 4
- iblank: int32 [32, 64, 4096], P('xi', 'eta', 'zeta'), may hold values 0 or 1
- speeds: float32 [3, 5], replicated, may hold values from -1.5 to 1.5
- transforms: float32 [4, 5, 5], replicated, as said below
- inv_xi: float32 [5, 32, 32], P(None, 'xi')
- inv_eta: float32 [5, 64, 64], P(None, 'eta')
- inv_zeta: float32 [5, 4096, 4096], P(None, 'zeta')
Outputs:
- residual: float32 [5, 32, 64, 4096], P(None, 'xi', 'eta', 'zeta')
- advanced: float32 [5, 32, 64, 4096], P(None, 'xi', 'eta', 'zeta')
The draws below stay inside these ranges and needn't reach their ends.
Inputs may be any that keep to these rules, and one draw needn't show every extreme that they name: transforms and line inverses are of order one with a unit diagonal part.
All inputs are finite; a program needn't handle non-finite values. No bound on the sum of `iblank` on one device may be relied on, other than what follows from the above.
Results may differ from the reference program's by a relative error of at most 0.000082.
Values sent between devices are 32-bit elements; how exact they have to be, the bound alone decides.
No kernel may reach another device: no remote copies, remote signals or barrier semaphores. Data moves between devices by JAX's collectives and lax.ppermute only.
A program may use at most 128 MiB of HBM per device.

```python
import math
import jax
import jax.numpy as jnp
from jax import lax

NV = 5
NX = 32
NY = 64
NZ = 4096


def line_inverse(key, length):
    eye = (jnp.arange(length)[:, None] == jnp.arange(length)[None, :]).astype(jnp.float32)
    noise = jax.random.normal(key, (NV, length, length), jnp.float32)
    return eye[None] + noise * (0.5 / length ** 0.5)


def draw_transforms(key, part):
    key = jax.random.fold_in(key, 11)
    eye = (jnp.arange(NV)[:, None] == jnp.arange(NV)[None, :]).astype(jnp.float32)
    noise = jax.random.normal(key, (4, NV, NV), jnp.float32) * 0.3
    return eye[None] + noise


def draw_inv_xi(key, part):
    key = jax.random.fold_in(key, 21)
    return line_inverse(key, NX)


def draw_inv_eta(key, part):
    key = jax.random.fold_in(key, 31)
    return line_inverse(key, NY)


def draw_inv_zeta(key, part):
    key = jax.random.fold_in(key, 41)
    return line_inverse(key, NZ)


def place_ends(values, key, least, largest):
    spot = [jax.random.randint(jax.random.fold_in(key, axis), (), 0, length) for axis, length in enumerate(values.shape)]
    longest = values.shape.index(max(values.shape))
    next_to = spot[:longest] + [(spot[longest] + 1) % values.shape[longest]] + spot[longest + 1:]
    return values.at[tuple(spot)].set(least).at[tuple(next_to)].set(largest)


def levels(rng, extent, shards, least, largest):
    gain = 1.0
    for position, blocks in shards:
        steps = jax.random.uniform(jax.random.fold_in(jax.random.fold_in(rng, 6), position), (blocks,), jnp.float32, least / len(shards), largest / len(shards))
        gain = gain * jnp.repeat(jnp.exp(steps), extent[position] // blocks).reshape((-1,) + (1,) * (len(extent) - 1 - position))
    return gain


def normal_values(stream_key, extent, scale, limit, shards=(), held_as=jnp.bfloat16):
    gain = levels(stream_key, extent, shards, -0.22, 0.18) if shards else 1.0
    array = jax.random.normal(stream_key, extent, jnp.float32) * scale * gain
    return jnp.minimum(jnp.maximum(array, -limit), limit).astype(held_as)


def setup_inputs(seed: int = 0) -> dict:
    splits = jax.random.split(jax.random.key(seed), 9)
    state = normal_values(splits[0], (NV, NX, NY, NZ), 1.0, 6.0, ((1, 4), (2, 2), (3, 32)), jnp.float32)
    radius = jnp.clip(jnp.exp(math.log(4.0) - 2.0794415 * jax.random.uniform(splits[1], (NX, NY, NZ), jnp.float32) ** levels(splits[1], (NX, NY, NZ), ((0, 4), (1, 2), (2, 32)), -0.2, 0.2)), 0.5, 4.0)
    iblank = place_ends((jax.random.randint(splits[2], (NX, NY, NZ), 0, 8) < 7).astype(jnp.int32), jax.random.fold_in(splits[2], 1), 0, 1)
    speeds = jnp.clip(jax.random.uniform(splits[3], (3, NV), jnp.float32, -1.5, 1.5), -1.5, 1.5)
    transforms = draw_transforms(jax.random.fold_in(splits[8], 71), 0)
    inv_xi = draw_inv_xi(jax.random.fold_in(splits[8], 71), 0)
    inv_eta = draw_inv_eta(jax.random.fold_in(splits[8], 71), 0)
    inv_zeta = draw_inv_zeta(jax.random.fold_in(splits[8], 71), 0)
    return {"state": state, "radius": radius, "iblank": iblank, "speeds": speeds, "transforms": transforms, "inv_xi": inv_xi, "inv_eta": inv_eta, "inv_zeta": inv_zeta}


HIGH = lax.Precision.HIGHEST


def shifted(padded, axis, offset):
    index = [slice(None), slice(2, -2), slice(2, -2), slice(2, -2)]
    index[axis] = slice(2 + offset, padded.shape[axis] - 2 + offset)
    return padded[tuple(index)]


def stencil(padded, speeds, radius, iblank):
    center = shifted(padded, 1, 0)
    total = jnp.zeros_like(center)
    for direction in range(3):
        axis = direction + 1
        up_one = shifted(padded, axis, 1)
        down_one = shifted(padded, axis, -1)
        up_two = shifted(padded, axis, 2)
        down_two = shifted(padded, axis, -2)
        flux = 0.5 * speeds[direction][:, None, None, None] * (up_one - down_one)
        diss = 0.04 * radius[None] * (up_two - 4.0 * up_one + 6.0 * center - 4.0 * down_one + down_two)
        total = total + flux + diss
    return -iblank.astype(jnp.float32)[None] * total


def mix(matrix, field):
    return jnp.einsum("ab,bxyz->axyz", matrix, field, precision=HIGH)


def reference(state, radius, iblank, speeds, transforms, inv_xi, inv_eta, inv_zeta):
    padded = jnp.pad(state, ((0, 0), (2, 2), (2, 2), (2, 2)))
    residual = stencil(padded, speeds, radius, iblank)
    work = mix(transforms[0], residual)
    work = jnp.einsum("vij,vjyz->viyz", inv_xi, work, precision=HIGH)
    work = mix(transforms[1], work)
    work = jnp.einsum("vjl,vxlz->vxjz", inv_eta, work, precision=HIGH)
    work = mix(transforms[2], work)
    work = jnp.einsum("vkl,vxyl->vxyk", inv_zeta, work, precision=HIGH)
    advanced = state + mix(transforms[3], work)
    return residual, advanced
```

```python
import functools

import jax
import jax.numpy as jnp
from jax import lax
from jax.experimental import pallas as pl
from jax.experimental.pallas import tpu as pltpu
from jax.sharding import PartitionSpec as P

F32 = jnp.float32
BF16 = jnp.bfloat16
SMEM = pl.BlockSpec(memory_space=pltpu.SMEM)
HBM = pl.BlockSpec(memory_space=pltpu.HBM)
VMEM = pl.BlockSpec()
NZC, NYC = 8, 4


def position():
    xi, eta, zeta = (lax.axis_index(name) for name in ("xi", "eta", "zeta"))
    return xi, eta, lax.div(zeta, 4), lax.rem(zeta, 4)


def shape(*dims, dtype=F32):
    return jax.ShapeDtypeStruct(dims, dtype)


def split(x):
    high = x.astype(BF16)
    low = (x - high.astype(F32)).astype(BF16)
    return high, low


def dot(a, b, dims):
    return lax.dot_general(a, b, (dims, ((), ())), preferred_element_type=F32)


def dot3(a, b, dims=((1,), (0,))):
    a_high, a_low = a
    b_high, b_low = b
    return dot(a_high, b_high, dims) + dot(a_high, b_low, dims) + dot(a_low, b_high, dims)


def mixed(t_ref, which, fields):
    out = []
    for a in range(5):
        total = t_ref[which, a, 0] * fields[0]
        for b in range(1, 5):
            total = total + t_ref[which, a, b] * fields[b]
        out.append(total)
    return out


def faces_kernel(state, xlo, xhi, yface, zlo, zhi):
    _, eta, _, _ = position()
    xlo[...] = state[:, 0:2]
    xhi[...] = state[:, 6:8]
    start = pl.multiple_of(24 * (1 - eta), 8)
    yface[...] = state[:, :, pl.ds(start, 8), :]
    for c in range(10):
        v, x = divmod(4 * c, 8)
        t = state[v, x : x + 4].reshape(128, 128).T
        zlo[:, 128 * c : 128 * (c + 1)] = t[0:8]
        zhi[:, 128 * c : 128 * (c + 1)] = t[120:128]


def faces(state):
    return pl.pallas_call(
        faces_kernel,
        in_specs=[VMEM],
        out_specs=[VMEM] * 5,
        out_shape=[
            shape(5, 2, 32, 128),
            shape(5, 2, 32, 128),
            shape(5, 8, 8, 128),
            shape(8, 1280),
            shape(8, 1280),
        ],
        name="faces",
    )(state)


def residual_kernel(
    speeds, t_ref, state, radius_hbm, iblank_hbm, inv_xi_hbm, xprev, xnext, yrec, zprev, znext,
    residual, m0, m1, m2, m3, ext, radius, iblank, inv_xi, zface, w0, sems,
):
    xi, eta, _, _ = position()
    copies = [
        pltpu.make_async_copy(state, ext.at[:, pl.ds(2, 8)], sems.at[0]),
        pltpu.make_async_copy(radius_hbm, radius, sems.at[1]),
        pltpu.make_async_copy(iblank_hbm, iblank, sems.at[2]),
        pltpu.make_async_copy(inv_xi_hbm, inv_xi, sems.at[3]),
    ]
    for copy in copies:
        copy.start()
    ext[:, 0:2] = xprev[...]
    ext[:, 10:12] = xnext[...]
    for c in range(10):
        v, x = divmod(4 * c, 8)
        lanes = slice(128 * c, 128 * (c + 1))
        t = jnp.concatenate([znext[:, lanes], jnp.zeros((112, 128), F32), zprev[:, lanes]], axis=0)
        zface[v, x : x + 4] = t.T.reshape(4, 32, 128)
    lane = lax.broadcasted_iota(jnp.int32, (32, 128), 1)
    row = lax.broadcasted_iota(jnp.int32, (32, 128), 0)
    has_low = eta == 1
    for copy in copies:
        copy.wait()

    def body(x, carry):
        rad = 0.04 * radius[x]
        keep = -iblank[x].astype(F32)
        fields = []
        for v in range(5):
            q = ext[v, x + 2]
            xp, xm = ext[v, x + 3], ext[v, x + 1]
            xpp, xmm = ext[v, x + 4], ext[v, x]
            face = yrec[v, x]
            lows = jnp.where(has_low, face, 0.0)
            highs = jnp.where(has_low, 0.0, face)
            l2, l1 = lows[6:7], lows[7:8]
            h1, h2 = highs[0:1], highs[1:2]
            yp = jnp.where(row == 31, h1, pltpu.roll(q, 31, 0))
            ypp = jnp.where(row == 31, h2, jnp.where(row == 30, h1, pltpu.roll(q, 30, 0)))
            ym = jnp.where(row == 0, l1, pltpu.roll(q, 1, 0))
            ymm = jnp.where(row == 0, l2, jnp.where(row == 1, l1, pltpu.roll(q, 2, 0)))
            z = zface[v, x]
            zp = pltpu.roll(jnp.where(lane == 0, z, q), 127, 1)
            zpp = pltpu.roll(jnp.where(lane < 2, z, q), 126, 1)
            zm = pltpu.roll(jnp.where(lane == 127, z, q), 1, 1)
            zmm = pltpu.roll(jnp.where(lane >= 126, z, q), 2, 1)
            flux = (
                (0.5 * speeds[0, v]) * (xp - xm)
                + (0.5 * speeds[1, v]) * (yp - ym)
                + (0.5 * speeds[2, v]) * (zp - zm)
            )
            far = (xpp + xmm) + (ypp + ymm) + (zpp + zmm)
            near = (xp + xm) + (yp + ym) + (zp + zm)
            diss = rad * (far - 4.0 * near + 18.0 * q)
            r = keep * (flux + diss)
            residual[v, x] = r
            fields.append(r)
        for v, value in enumerate(mixed(t_ref, 0, fields)):
            w0[v, x] = value
        return carry

    lax.fori_loop(0, 8, body, 0)
    for s, m in enumerate((m0, m1, m2, m3)):
        start = pl.multiple_of(8 * lax.rem(xi + s, 4), 8)
        m[:, 0:8] = w0[:, :, pl.ds(start, 8), :]
        m[:, 8] = jnp.concatenate([inv_xi[...], jnp.zeros((5, 8, 96), F32)], axis=2)


def residual_step(speeds, transforms, *arrays):
    return pl.pallas_call(
        residual_kernel,
        in_specs=[SMEM] * 2 + [HBM] * 4 + [VMEM] * 5,
        out_specs=[VMEM] * 5,
        out_shape=[shape(5, 8, 32, 128)] + [shape(5, 9, 8, 128)] * 4,
        scratch_shapes=[
            pltpu.VMEM((5, 12, 32, 128), F32),
            pltpu.VMEM((8, 32, 128), F32),
            pltpu.VMEM((8, 32, 128), jnp.int32),
            pltpu.VMEM((5, 8, 32), F32),
            pltpu.VMEM((5, 8, 32, 128), F32),
            pltpu.VMEM((5, 8, 32, 128), F32),
            pltpu.SemaphoreType.DMA((4,)),
        ],
        compiler_params=pltpu.CompilerParams(vmem_limit_bytes=16 << 20),
        name="residual",
    )(speeds, transforms, *arrays)


def xi_kernel(t_ref, r0, r1, r2, r3, b0, b1, b2, b3, field, inverse, work):
    xi, _, _, _ = position()
    for s, r in enumerate((r0, r1, r2, r3)):
        start = pl.multiple_of(8 * lax.rem(xi + 4 - s, 4), 8)
        field[:, pl.ds(start, 8)] = r[:, 0:8]
        inverse[:, pl.ds(start, 8), :] = r[:, 8]
    rows = lax.broadcasted_iota(jnp.int32, (256, 32), 0) // 8
    spread = (rows == lax.broadcasted_iota(jnp.int32, (256, 32), 1)).astype(F32).astype(BF16)
    cols = lax.broadcasted_iota(jnp.int32, (128, 256), 1) // 8
    widen = (cols == lax.broadcasted_iota(jnp.int32, (128, 256), 0)).astype(F32).astype(BF16)
    same = (
        lax.broadcasted_iota(jnp.int32, (256, 256), 0) % 8
        == lax.broadcasted_iota(jnp.int32, (256, 256), 1) % 8
    )
    for v in range(5):
        line = []
        for part in split(inverse[v]):
            wide = dot(part, widen, ((1,), (0,))).astype(BF16)
            full = dot(spread, wide, ((1,), (0,)))
            line.append(jnp.where(same, full, 0.0).astype(BF16))
        value = dot3(line, split(field[v].reshape(256, 128)))
        work[v] = value.reshape(32, 8, 128)

    def body(x, carry):
        for v, value in enumerate(mixed(t_ref, 1, [work[v, x] for v in range(5)])):
            field[v, x] = value
        return carry

    lax.fori_loop(0, 32, body, 0)
    for s, b in enumerate((b0, b1, b2, b3)):
        b[...] = field[:, pl.ds(8 * lax.rem(xi + s, 4), 8)]


def xi_step(transforms, parts):
    return pl.pallas_call(
        xi_kernel,
        in_specs=[SMEM] + [VMEM] * 4,
        out_specs=[VMEM] * 4,
        out_shape=[shape(5, 8, 8, 128)] * 4,
        scratch_shapes=[
            pltpu.VMEM((5, 32, 8, 128), F32),
            pltpu.VMEM((5, 32, 128), F32),
            pltpu.VMEM((5, 32, 8, 128), F32),
        ],
        compiler_params=pltpu.CompilerParams(vmem_limit_bytes=16 << 20),
        name="xi_lines",
    )(transforms, *parts)


def eta_kernel(t_ref, inv_eta, p0, p1, p2, p3, q0, q1, q2, q3, out, field, work):
    xi, eta, _, _ = position()
    for s, (p, q) in enumerate(zip((p0, p1, p2, p3), (q0, q1, q2, q3))):
        rows = 8 * lax.rem(xi + 4 - s, 4)
        field[:, :, pl.ds(pl.multiple_of(32 * eta + rows, 8), 8), :] = p[...]
        field[:, :, pl.ds(pl.multiple_of(32 * (1 - eta) + rows, 8), 8), :] = q[...]
    for v in range(5):
        wide = jnp.concatenate([field[v, x] for x in range(8)], axis=1)
        value = dot3(split(inv_eta[v]), split(wide))
        for x in range(8):
            work[v, x] = value[:, 128 * x : 128 * (x + 1)]


    def body(x, carry):
        for v, value in enumerate(mixed(t_ref, 2, [work[v, x] for v in range(5)])):
            out[v, x] = value
        return carry

    lax.fori_loop(0, 8, body, 0)


def eta_step(transforms, inv_eta, own, other):
    return pl.pallas_call(
        eta_kernel,
        in_specs=[SMEM] + [VMEM] * 9,
        out_specs=VMEM,
        out_shape=shape(5, 8, 32, 128),
        scratch_shapes=[pltpu.VMEM((5, 8, 64, 128), F32), pltpu.VMEM((5, 8, 32, 128), F32)],
        compiler_params=pltpu.CompilerParams(vmem_limit_bytes=16 << 20),
        name="eta_lines",
    )(transforms, inv_eta, *own, *other)


def pick_kernel(inv, g1, g2, g3, lines, sems):
    _, eta, _, y = position()
    rows = pl.ds(pl.multiple_of(64 * eta, 64), 64)
    copies = [
        pltpu.make_async_copy(inv.at[v, rows], lines.at[v], sems.at[v]) for v in range(5)
    ]
    for copy in copies:
        copy.start()
    for v, copy in enumerate(copies):
        copy.wait()
        for s, g in enumerate((g1, g2, g3)):
            for z in range(NZC):
                lanes = pl.multiple_of(512 * z + 128 * lax.rem(y + s + 1, 4), 128)
                g[z, v] = lines[v, :, pl.ds(lanes, 128)]


def pick(inv_zeta):
    return pl.pallas_call(
        pick_kernel,
        in_specs=[HBM],
        out_specs=[VMEM] * 3,
        out_shape=[shape(NZC, 5, 64, 128)] * 3,
        scratch_shapes=[pltpu.VMEM((5, 64, 4096), F32), pltpu.SemaphoreType.DMA((5,))],
        compiler_params=pltpu.CompilerParams(vmem_limit_bytes=56 << 20),
        name="pick",
    )(inv_zeta)


def prepare_kernel(inv, h1, h2, h3, o1, o2, o3, high, low):
    _, eta, _, y = position()
    for z in range(NZC):
        lanes = slice(128 * z, 128 * (z + 1))
        own = inv[0, :, pl.ds(pl.multiple_of(512 * z + 128 * y, 128), 128)]
        high[0, 0, :, lanes], low[0, 0, :, lanes] = split(own)
        for c, (h, o) in enumerate(((h1, o1), (h2, o2), (h3, o3))):
            for half, part in ((eta, h), (1 - eta, o)):
                rows = pl.ds(pl.multiple_of(64 * half, 64), 64)
                high[0, c + 1, rows, lanes], low[0, c + 1, rows, lanes] = split(part[z, 0])


def prepare(inv_zeta, own_halves, other_halves):
    half = pl.BlockSpec((NZC, 1, 64, 128), lambda v: (0, v, 0, 0))
    return pl.pallas_call(
        prepare_kernel,
        grid=(5,),
        in_specs=[pl.BlockSpec((1, 128, 4096), lambda v: (v, 0, 0))] + [half] * 6,
        out_specs=[pl.BlockSpec((1, 4, 128, 1024), lambda v: (v, 0, 0, 0))] * 2,
        out_shape=[shape(5, 4, 128, 1024, dtype=BF16)] * 2,
        compiler_params=pltpu.CompilerParams(vmem_limit_bytes=24 << 20),
        name="prepare",
    )(inv_zeta, *own_halves, *other_halves)


def zeta_kernel(b_ref, high, low, *outs):
    b = split(jnp.concatenate([b_ref[z, 0].reshape(256, 128) for z in range(NZC)], axis=1))
    for c in range(4):
        outs[c][0] = dot3(b, (high[0, c], low[0, c]), ((1,), (1,)))


def zeta_step(gathered, high, low):
    lines = pl.BlockSpec((1, 4, 128, 1024), lambda v: (v, 0, 0, 0))
    return pl.pallas_call(
        zeta_kernel,
        grid=(5,),
        in_specs=[pl.BlockSpec((NZC, 1, 8, 32, 128), lambda v: (0, v, 0, 0, 0)), lines, lines],
        out_specs=[pl.BlockSpec((1, 256, 128), lambda v: (v, 0, 0))] * 4,
        out_shape=[shape(5, 256, 128)] * 4,
        compiler_params=pltpu.CompilerParams(vmem_limit_bytes=56 << 20),
        name="zeta_lines",
    )(gathered, high, low)


def final_kernel(t_ref, state, c0, c1, c2, c3, out):
    def body(x, carry):
        fields = [c0[v, x] + c1[v, x] + c2[v, x] + c3[v, x] for v in range(5)]
        for v, value in enumerate(mixed(t_ref, 3, fields)):
            out[v, x] = state[v, x] + value
        return carry

    lax.fori_loop(0, 8, body, 0)


def final_step(transforms, state, parts):
    return pl.pallas_call(
        final_kernel,
        in_specs=[SMEM] + [VMEM] * 5,
        out_specs=VMEM,
        out_shape=shape(5, 8, 32, 128),
        compiler_params=pltpu.CompilerParams(vmem_limit_bytes=16 << 20),
        name="final",
    )(transforms, state, *parts)


def over_x(array, s):
    return lax.ppermute(array, "xi", [(i, (i + s) % 4) for i in range(4)])


def over_y(array, s):
    pairs = [(4 * z + y, 4 * z + (y + s) % 4) for z in range(NZC) for y in range(NYC)]
    return lax.ppermute(array, "zeta", pairs)


def over_core(array):
    return lax.ppermute(array, "eta", [(0, 1), (1, 0)])


def shift_line(array, axis, s):
    size = lax.axis_size(axis)
    pairs = [(i, i + s) for i in range(size) if 0 <= i + s < size]
    return lax.ppermute(array, axis, pairs)


def after(array, *first):
    return lax.optimization_barrier((array, *first))[0]


def local(state, radius, iblank, speeds, transforms, inv_xi, inv_eta, inv_zeta):
    xlo, xhi, yface, zlo, zhi = faces(state)
    halos = [
        shift_line(xhi, "xi", 1),
        shift_line(xlo, "xi", -1),
        over_core(yface),
        shift_line(zhi, "zeta", 1),
        shift_line(zlo, "zeta", -1),
    ]
    g1, g2, g3 = pick(inv_zeta)
    halos[0] = after(halos[0], g1)
    residual, m0, m1, m2, m3 = residual_step(
        speeds, transforms, state, radius, iblank, inv_xi, *halos
    )
    h1, h3 = over_y(after(g1, m0), 1), over_y(after(g3, m0), 3)
    parts = [m0] + [over_x(m, s + 1) for s, m in enumerate((m1, m2, m3))]
    b0, b1, b2, b3 = xi_step(transforms, parts)
    own = [b0] + [over_x(b, s + 1) for s, b in enumerate((b1, b2, b3))]
    other = [over_core(p) for p in own]
    own[0] = after(own[0], h1, h3)
    h2 = over_y(after(g2, h1, h3, own[1]), 2)
    work = eta_step(transforms, inv_eta, own, other)

    columns = [[4 * z + y for z in range(NZC)] for y in range(NYC)]
    gathered = lax.all_gather(work, "zeta", axis_index_groups=columns)
    own_halves = (h1, h2, h3)
    other_halves = [over_core(after(h, work)) for h in own_halves]
    high, low = prepare(inv_zeta, own_halves, other_halves)
    c0, c1, c2, c3 = zeta_step(gathered, high, low)
    back = [c0] + [over_y(c, -(s + 1)) for s, c in enumerate((c1, c2, c3))]
    advanced = final_step(transforms, state, [c.reshape(5, 8, 32, 128) for c in back])
    return residual, advanced


def solution(mesh):
    placed = (
        P(None, "xi", "eta", "zeta"),
        P("xi", "eta", "zeta"),
        P("xi", "eta", "zeta"),
        P(),
        P(),
        P(None, "xi", None),
        P(None, "eta", None),
        P(None, "zeta", None),
    )
    return jax.shard_map(
        local,
        mesh=mesh,
        in_specs=placed,
        out_specs=(P(None, "xi", "eta", "zeta"), P(None, "xi", "eta", "zeta")),
        check_vma=False,
    )
```

```python
import functools

import jax
import jax.numpy as jnp
from jax import lax
from jax.experimental import pallas as pl
from jax.experimental.pallas import tpu as pltpu
from jax.sharding import PartitionSpec as P

F32 = jnp.float32
BF16 = jnp.bfloat16
SMEM = pl.BlockSpec(memory_space=pltpu.SMEM)
HBM = pl.BlockSpec(memory_space=pltpu.HBM)
VMEM = pl.BlockSpec()
NZC, NYC = 8, 4
PICKED_STEP = (2, 2, 1, 3)
PICKED_FIRST = (0, 3, 0, 0)
PICKED_COUNT = (3, 2, 5, 5)


def position():
    xi, eta, zeta = (lax.axis_index(name) for name in ("xi", "eta", "zeta"))
    return xi, eta, lax.div(zeta, 4), lax.rem(zeta, 4)


def shape(*dims, dtype=F32):
    return jax.ShapeDtypeStruct(dims, dtype)


def split(x):
    high = x.astype(BF16)
    low = (x - high.astype(F32)).astype(BF16)
    return high, low


def dot(a, b, dims):
    return lax.dot_general(a, b, (dims, ((), ())), preferred_element_type=F32)


def dot3(a, b, dims=((1,), (0,))):
    a_high, a_low = a
    b_high, b_low = b
    return dot(a_high, b_high, dims) + dot(a_high, b_low, dims) + dot(a_low, b_high, dims)


def mixed(t_ref, which, fields):
    out = []
    for a in range(5):
        total = t_ref[which, a, 0] * fields[0]
        for b in range(1, 5):
            total = total + t_ref[which, a, b] * fields[b]
        out.append(total)
    return out


def faces_kernel(state, xlo, xhi, yface, zlo, zhi):
    _, eta, _, _ = position()
    xlo[...] = state[:, 0:2]
    xhi[...] = state[:, 6:8]
    start = pl.multiple_of(24 * (1 - eta), 8)
    yface[...] = state[:, :, pl.ds(start, 8), :]
    for c in range(10):
        v, x = divmod(4 * c, 8)
        t = state[v, x : x + 4].reshape(128, 128).T
        zlo[:, 128 * c : 128 * (c + 1)] = t[0:8]
        zhi[:, 128 * c : 128 * (c + 1)] = t[120:128]


def faces(state):
    return pl.pallas_call(
        faces_kernel,
        in_specs=[VMEM],
        out_specs=[VMEM] * 5,
        out_shape=[
            shape(5, 2, 32, 128),
            shape(5, 2, 32, 128),
            shape(5, 8, 8, 128),
            shape(8, 1280),
            shape(8, 1280),
        ],
        name="faces",
    )(state)


def residual_kernel(
    speeds, t_ref, state, radius_hbm, iblank_hbm, inv_xi_hbm, xprev, xnext, yrec, zprev, znext,
    residual, m0, m1, m2, m3, ext, radius, iblank, inv_xi, zface, w0, sems,
):
    xi, eta, _, _ = position()
    copies = [
        pltpu.make_async_copy(state, ext.at[:, pl.ds(2, 8)], sems.at[0]),
        pltpu.make_async_copy(radius_hbm, radius, sems.at[1]),
        pltpu.make_async_copy(iblank_hbm, iblank, sems.at[2]),
        pltpu.make_async_copy(inv_xi_hbm, inv_xi, sems.at[3]),
    ]
    for copy in copies:
        copy.start()
    ext[:, 0:2] = xprev[...]
    ext[:, 10:12] = xnext[...]
    for c in range(10):
        v, x = divmod(4 * c, 8)
        lanes = slice(128 * c, 128 * (c + 1))
        t = jnp.concatenate([znext[:, lanes], jnp.zeros((112, 128), F32), zprev[:, lanes]], axis=0)
        zface[v, x : x + 4] = t.T.reshape(4, 32, 128)
    lane = lax.broadcasted_iota(jnp.int32, (32, 128), 1)
    row = lax.broadcasted_iota(jnp.int32, (32, 128), 0)
    has_low = eta == 1
    for copy in copies:
        copy.wait()

    def body(x, carry):
        rad = 0.04 * radius[x]
        keep = -iblank[x].astype(F32)
        fields = []
        for v in range(5):
            q = ext[v, x + 2]
            xp, xm = ext[v, x + 3], ext[v, x + 1]
            xpp, xmm = ext[v, x + 4], ext[v, x]
            face = yrec[v, x]
            lows = jnp.where(has_low, face, 0.0)
            highs = jnp.where(has_low, 0.0, face)
            l2, l1 = lows[6:7], lows[7:8]
            h1, h2 = highs[0:1], highs[1:2]
            yp = jnp.where(row == 31, h1, pltpu.roll(q, 31, 0))
            ypp = jnp.where(row == 31, h2, jnp.where(row == 30, h1, pltpu.roll(q, 30, 0)))
            ym = jnp.where(row == 0, l1, pltpu.roll(q, 1, 0))
            ymm = jnp.where(row == 0, l2, jnp.where(row == 1, l1, pltpu.roll(q, 2, 0)))
            z = zface[v, x]
            zp = pltpu.roll(jnp.where(lane == 0, z, q), 127, 1)
            zpp = pltpu.roll(jnp.where(lane < 2, z, q), 126, 1)
            zm = pltpu.roll(jnp.where(lane == 127, z, q), 1, 1)
            zmm = pltpu.roll(jnp.where(lane >= 126, z, q), 2, 1)
            flux = (
                (0.5 * speeds[0, v]) * (xp - xm)
                + (0.5 * speeds[1, v]) * (yp - ym)
                + (0.5 * speeds[2, v]) * (zp - zm)
            )
            far = (xpp + xmm) + (ypp + ymm) + (zpp + zmm)
            near = (xp + xm) + (yp + ym) + (zp + zm)
            diss = rad * (far - 4.0 * near + 18.0 * q)
            r = keep * (flux + diss)
            residual[v, x] = r
            fields.append(r)
        for v, value in enumerate(mixed(t_ref, 0, fields)):
            w0[v, x] = value
        return carry

    lax.fori_loop(0, 8, body, 0)
    for s, m in enumerate((m0, m1, m2, m3)):
        start = pl.multiple_of(8 * lax.rem(xi + s, 4), 8)
        m[:, 0:8] = w0[:, :, pl.ds(start, 8), :]
        m[:, 8] = jnp.concatenate([inv_xi[...], jnp.zeros((5, 8, 96), F32)], axis=2)


def residual_step(speeds, transforms, *arrays):
    return pl.pallas_call(
        residual_kernel,
        in_specs=[SMEM] * 2 + [HBM] * 4 + [VMEM] * 5,
        out_specs=[VMEM] * 5,
        out_shape=[shape(5, 8, 32, 128)] + [shape(5, 9, 8, 128)] * 4,
        scratch_shapes=[
            pltpu.VMEM((5, 12, 32, 128), F32),
            pltpu.VMEM((8, 32, 128), F32),
            pltpu.VMEM((8, 32, 128), jnp.int32),
            pltpu.VMEM((5, 8, 32), F32),
            pltpu.VMEM((5, 8, 32, 128), F32),
            pltpu.VMEM((5, 8, 32, 128), F32),
            pltpu.SemaphoreType.DMA((4,)),
        ],
        compiler_params=pltpu.CompilerParams(vmem_limit_bytes=16 << 20),
        name="residual",
    )(speeds, transforms, *arrays)


def xi_kernel(t_ref, r0, r1, r2, r3, b0, b1, b2, b3, field, inverse, work):
    xi, _, _, _ = position()
    for s, r in enumerate((r0, r1, r2, r3)):
        start = pl.multiple_of(8 * lax.rem(xi + 4 - s, 4), 8)
        field[:, pl.ds(start, 8)] = r[:, 0:8]
        inverse[:, pl.ds(start, 8), :] = r[:, 8]
    rows = lax.broadcasted_iota(jnp.int32, (256, 32), 0) // 8
    spread = (rows == lax.broadcasted_iota(jnp.int32, (256, 32), 1)).astype(F32).astype(BF16)
    cols = lax.broadcasted_iota(jnp.int32, (128, 256), 1) // 8
    widen = (cols == lax.broadcasted_iota(jnp.int32, (128, 256), 0)).astype(F32).astype(BF16)
    same = (
        lax.broadcasted_iota(jnp.int32, (256, 256), 0) % 8
        == lax.broadcasted_iota(jnp.int32, (256, 256), 1) % 8
    )
    for v in range(5):
        line = []
        for part in split(inverse[v]):
            wide = dot(part, widen, ((1,), (0,))).astype(BF16)
            full = dot(spread, wide, ((1,), (0,)))
            line.append(jnp.where(same, full, 0.0).astype(BF16))
        value = dot3(line, split(field[v].reshape(256, 128)))
        work[v] = value.reshape(32, 8, 128)

    def body(x, carry):
        for v, value in enumerate(mixed(t_ref, 1, [work[v, x] for v in range(5)])):
            field[v, x] = value
        return carry

    lax.fori_loop(0, 32, body, 0)
    for s, b in enumerate((b0, b1, b2, b3)):
        b[...] = field[:, pl.ds(8 * lax.rem(xi + s, 4), 8)]


def xi_step(transforms, parts):
    return pl.pallas_call(
        xi_kernel,
        in_specs=[SMEM] + [VMEM] * 4,
        out_specs=[VMEM] * 4,
        out_shape=[shape(5, 8, 8, 128)] * 4,
        scratch_shapes=[
            pltpu.VMEM((5, 32, 8, 128), F32),
            pltpu.VMEM((5, 32, 128), F32),
            pltpu.VMEM((5, 32, 8, 128), F32),
        ],
        compiler_params=pltpu.CompilerParams(vmem_limit_bytes=16 << 20),
        name="xi_lines",
    )(transforms, *parts)


def eta_kernel(t_ref, inv_eta, p0, p1, p2, p3, q0, q1, q2, q3, out, field, work):
    xi, eta, _, _ = position()
    for s, (p, q) in enumerate(zip((p0, p1, p2, p3), (q0, q1, q2, q3))):
        rows = 8 * lax.rem(xi + 4 - s, 4)
        field[:, :, pl.ds(pl.multiple_of(32 * eta + rows, 8), 8), :] = p[...]
        field[:, :, pl.ds(pl.multiple_of(32 * (1 - eta) + rows, 8), 8), :] = q[...]
    for v in range(5):
        wide = jnp.concatenate([field[v, x] for x in range(8)], axis=1)
        value = dot3(split(inv_eta[v]), split(wide))
        for x in range(8):
            work[v, x] = value[:, 128 * x : 128 * (x + 1)]


    def body(x, carry):
        for v, value in enumerate(mixed(t_ref, 2, [work[v, x] for v in range(5)])):
            out[v, x] = value
        return carry

    lax.fori_loop(0, 8, body, 0)


def eta_step(transforms, inv_eta, own, other):
    return pl.pallas_call(
        eta_kernel,
        in_specs=[SMEM] + [VMEM] * 9,
        out_specs=VMEM,
        out_shape=shape(5, 8, 32, 128),
        scratch_shapes=[pltpu.VMEM((5, 8, 64, 128), F32), pltpu.VMEM((5, 8, 32, 128), F32)],
        compiler_params=pltpu.CompilerParams(vmem_limit_bytes=16 << 20),
        name="eta_lines",
    )(transforms, inv_eta, *own, *other)


def pick_kernel(inv, *refs):
    _, eta, _, y = position()
    *outs, lines, sems = refs
    rows = pl.ds(pl.multiple_of(64 * eta, 64), 64)
    copies = [
        pltpu.make_async_copy(inv.at[v, rows], lines.at[v], sems.at[v]) for v in range(5)
    ]
    for copy in copies:
        copy.start()
    for v, copy in enumerate(copies):
        copy.wait()
        for s, first, count, g in zip(PICKED_STEP, PICKED_FIRST, PICKED_COUNT, outs):
            if first <= v < first + count:
                for z in range(NZC):
                    lanes = pl.multiple_of(512 * z + 128 * lax.rem(y + s, 4), 128)
                    g[z, v - first] = lines[v, :, pl.ds(lanes, 128)]


def pick(inv_zeta):
    return pl.pallas_call(
        pick_kernel,
        in_specs=[HBM],
        out_specs=[VMEM] * 4,
        out_shape=[shape(NZC, count, 64, 128) for count in PICKED_COUNT],
        scratch_shapes=[pltpu.VMEM((5, 64, 4096), F32), pltpu.SemaphoreType.DMA((5,))],
        compiler_params=pltpu.CompilerParams(vmem_limit_bytes=56 << 20),
        name="pick",
    )(inv_zeta)


def own_kernel(inv, high, low):
    _, _, _, y = position()
    for z in range(NZC):
        block = inv[0, :, pl.ds(pl.multiple_of(512 * z + 128 * y, 128), 128)]
        rows = slice(128 * z, 128 * (z + 1))
        high[0, rows], low[0, rows] = split(block.T)


def prepare_own(inv_zeta):
    return pl.pallas_call(
        own_kernel,
        grid=(5,),
        in_specs=[pl.BlockSpec((1, 128, 4096), lambda v: (v, 0, 0))],
        out_specs=[pl.BlockSpec((1, 1024, 128), lambda v: (v, 0, 0))] * 2,
        out_shape=[shape(5, 1024, 128, dtype=BF16)] * 2,
        compiler_params=pltpu.CompilerParams(vmem_limit_bytes=24 << 20),
        name="prepare_own",
    )(inv_zeta)


def prepare_kernel(*refs):
    _, eta, _, _ = position()
    own_parts, other_parts, (high2, low2, high, low, lines) = refs[:4], refs[4:8], refs[8:]
    v = pl.program_id(0)

    def place(index, own, other):
        for half, part in ((eta, own), (1 - eta, other)):
            rows = pl.ds(pl.multiple_of(64 * half, 64), 64)
            for z in range(NZC):
                lines[PICKED_STEP[index] - 1, rows, 128 * z : 128 * (z + 1)] = part[z, 0]

    for index, (own, other) in enumerate(zip(own_parts, other_parts)):
        first, count = PICKED_FIRST[index], PICKED_COUNT[index]
        if count == 5:
            place(index, own, other)
        else:
            held = jnp.logical_and(v >= first, v < first + count)
            pl.when(held)(functools.partial(place, index, own, other))
    for z in range(NZC):
        rows = slice(128 * z, 128 * (z + 1))
        high2[0, rows], low2[0, rows] = split(lines[1, :, rows].T)
        for c in range(2):
            lanes = slice(128 * c, 128 * (c + 1))
            high[0, rows, lanes], low[0, rows, lanes] = split(lines[2 * c, :, rows].T)


def prepare(own_parts, other_parts):
    widths = (128, 128, 256, 256)

    def part(first, count):
        return pl.BlockSpec(
            (NZC, 1, 64, 128), lambda v: (0, jnp.clip(v - first, 0, count - 1), 0, 0)
        )

    parts = [part(*pair) for pair in zip(PICKED_FIRST, PICKED_COUNT)]
    return pl.pallas_call(
        prepare_kernel,
        grid=(5,),
        in_specs=parts * 2,
        out_specs=[pl.BlockSpec((1, 1024, w), lambda v: (v, 0, 0)) for w in widths],
        out_shape=[shape(5, 1024, w, dtype=BF16) for w in widths],
        scratch_shapes=[pltpu.VMEM((3, 128, 1024), F32)],
        compiler_params=pltpu.CompilerParams(vmem_limit_bytes=24 << 20),
        name="prepare",
    )(*own_parts, *other_parts)


def zeta_kernel(count, b_ref, *refs):
    b = split(jnp.concatenate([b_ref[z, 0].reshape(256, 128) for z in range(NZC)], axis=1))
    outs = list(refs[2 * count :])
    for high, low in zip(refs[0 : 2 * count : 2], refs[1 : 2 * count : 2]):
        value = dot3(b, (high[0], low[0]))
        for place in range(high.shape[2] // 128):
            lanes = slice(128 * place, 128 * (place + 1))
            outs.pop(0)[0] = value[:128, lanes]
            outs.pop(0)[0] = value[128:, lanes]


def zeta_step(gathered, *lines):
    widths = [array.shape[2] for array in lines]
    count = sum(widths) // 128
    return pl.pallas_call(
        functools.partial(zeta_kernel, len(lines) // 2),
        grid=(5,),
        in_specs=[pl.BlockSpec((NZC, 1, 8, 32, 128), lambda v: (0, v, 0, 0, 0))]
        + [pl.BlockSpec((1, 1024, w), lambda v: (v, 0, 0)) for w in widths],
        out_specs=[pl.BlockSpec((1, 128, 128), lambda v: (v, 0, 0))] * count,
        out_shape=[shape(5, 128, 128)] * count,
        compiler_params=pltpu.CompilerParams(vmem_limit_bytes=48 << 20),
        name="zeta_lines",
    )(gathered, *lines)


def final_kernel(t_ref, state, own0, own1, low0, low1, high0, high1, out):
    for half, parts in enumerate(((own0, low0, high0), (own1, low1, high1))):

        def body(x, carry):
            rows = pl.ds(pl.multiple_of(32 * x, 32), 32)
            fields = [sum(part[v, rows] for part in parts) for v in range(5)]
            for v, value in enumerate(mixed(t_ref, 3, fields)):
                out[v, 4 * half + x] = state[v, 4 * half + x] + value
            return carry

        lax.fori_loop(0, 4, body, 0)


def final_step(transforms, state, parts):
    return pl.pallas_call(
        final_kernel,
        in_specs=[SMEM] + [VMEM] * 7,
        out_specs=VMEM,
        out_shape=shape(5, 8, 32, 128),
        compiler_params=pltpu.CompilerParams(vmem_limit_bytes=56 << 20),
        name="final",
    )(transforms, state, *parts)


def over_x(array, s):
    return lax.ppermute(array, "xi", [(i, (i + s) % 4) for i in range(4)])


def over_y(array, s):
    pairs = [(4 * z + y, 4 * z + (y + s) % 4) for z in range(NZC) for y in range(NYC)]
    return lax.ppermute(array, "zeta", pairs)


def over_core(array):
    return lax.ppermute(array, "eta", [(0, 1), (1, 0)])


def shift_line(array, axis, s):
    size = lax.axis_size(axis)
    pairs = [(i, i + s) for i in range(size) if 0 <= i + s < size]
    return lax.ppermute(array, axis, pairs)


def after(array, *first):
    return lax.optimization_barrier((array, *first))[0]


def local(state, radius, iblank, speeds, transforms, inv_xi, inv_eta, inv_zeta):
    xlo, xhi, yface, zlo, zhi = faces(state)
    halos = [
        shift_line(xhi, "xi", 1),
        shift_line(xlo, "xi", -1),
        over_core(yface),
        shift_line(zhi, "zeta", 1),
        shift_line(zlo, "zeta", -1),
    ]
    picked = pick(inv_zeta)
    halos[0] = after(halos[0], picked[0])
    residual, m0, m1, m2, m3 = residual_step(
        speeds, transforms, state, radius, iblank, inv_xi, *halos
    )
    parts = [m0] + [over_x(m, s + 1) for s, m in enumerate((m1, m2, m3))]
    sent = [over_y(after(picked[0], m0), PICKED_STEP[0])]
    b0, b1, b2, b3 = xi_step(transforms, parts)
    own = [b0] + [over_x(b, s + 1) for s, b in enumerate((b1, b2, b3))]
    other = [over_core(p) for p in own]
    own[0] = after(own[0], *sent)
    work = eta_step(transforms, inv_eta, own, other)

    columns = [[4 * z + y for z in range(NZC)] for y in range(NYC)]
    gathered = lax.all_gather(work, "zeta", axis_index_groups=columns)
    sent += [over_y(after(picked[i], work), PICKED_STEP[i]) for i in range(1, 4)]
    own_lines = prepare_own(after(inv_zeta, work))
    swapped = [over_core(after(part, *own_lines)) for part in sent]
    high2, low2, high, low = prepare(sent, swapped)

    far0, far1 = zeta_step(gathered, high2, low2)
    far0, far1 = over_y(far0, 1), over_y(far1, -1)
    down0, down1, up0, up1, own0, own1 = zeta_step(gathered, high, low, *own_lines)
    up1, down0 = over_y(up1, 1), over_y(down0, -1)
    up0, down1 = over_y(up0 + far0, 1), over_y(down1 + far1, -1)
    advanced = final_step(transforms, state, (own0, own1, up0, up1, down0, down1))
    return residual, advanced


def solution(mesh):
    placed = (
        P(None, "xi", "eta", "zeta"),
        P("xi", "eta", "zeta"),
        P("xi", "eta", "zeta"),
        P(),
        P(),
        P(None, "xi", None),
        P(None, "eta", None),
        P(None, "zeta", None),
    )
    return jax.shard_map(
        local,
        mesh=mesh,
        in_specs=placed,
        out_specs=(P(None, "xi", "eta", "zeta"), P(None, "xi", "eta", "zeta")),
        check_vma=False,
    )
```

```python
import functools

import jax
import jax.numpy as jnp
from jax import lax
from jax.experimental import pallas as pl
from jax.experimental.pallas import tpu as pltpu
from jax.sharding import PartitionSpec as P

F32 = jnp.float32
BF16 = jnp.bfloat16
SMEM = pl.BlockSpec(memory_space=pltpu.SMEM)
HBM = pl.BlockSpec(memory_space=pltpu.HBM)
VMEM = pl.BlockSpec()
NZC, NYC = 8, 4
PICKED_STEP = (2, 2, 1, 3)
PICKED_FIRST = (0, 3, 0, 0)
PICKED_COUNT = (3, 2, 5, 5)


def position():
    xi, eta, zeta = (lax.axis_index(name) for name in ("xi", "eta", "zeta"))
    return xi, eta, lax.div(zeta, 4), lax.rem(zeta, 4)


def shape(*dims, dtype=F32):
    return jax.ShapeDtypeStruct(dims, dtype)


def split(x):
    high = x.astype(BF16)
    low = (x - high.astype(F32)).astype(BF16)
    return high, low


def dot(a, b, dims):
    return lax.dot_general(a, b, (dims, ((), ())), preferred_element_type=F32)


def dot3(a, b, dims=((1,), (0,))):
    a_high, a_low = a
    b_high, b_low = b
    return dot(a_high, b_high, dims) + dot(a_high, b_low, dims) + dot(a_low, b_high, dims)


def mixed(t_ref, which, fields):
    out = []
    for a in range(5):
        total = t_ref[which, a, 0] * fields[0]
        for b in range(1, 5):
            total = total + t_ref[which, a, b] * fields[b]
        out.append(total)
    return out


def faces_kernel(state, xlo, xhi, yface, zlo, zhi):
    _, eta, _, _ = position()
    xlo[...] = state[:, 0:2]
    xhi[...] = state[:, 6:8]
    start = pl.multiple_of(24 * (1 - eta), 8)
    yface[...] = state[:, :, pl.ds(start, 8), :]
    for c in range(10):
        v, x = divmod(4 * c, 8)
        t = state[v, x : x + 4].reshape(128, 128).T
        zlo[:, 128 * c : 128 * (c + 1)] = t[0:8]
        zhi[:, 128 * c : 128 * (c + 1)] = t[120:128]


def faces(state):
    return pl.pallas_call(
        faces_kernel,
        in_specs=[VMEM],
        out_specs=[VMEM] * 5,
        out_shape=[
            shape(5, 2, 32, 128),
            shape(5, 2, 32, 128),
            shape(5, 8, 8, 128),
            shape(8, 1280),
            shape(8, 1280),
        ],
        name="faces",
    )(state)


def residual_kernel(
    speeds, t_ref, state, radius_hbm, iblank_hbm, inv_xi_hbm, xprev, xnext, yrec, zprev, znext,
    residual, m0, m1, m2, m3, ext, radius, iblank, inv_xi, zface, w0, sems,
):
    xi, eta, _, _ = position()
    copies = [
        pltpu.make_async_copy(state, ext.at[:, pl.ds(2, 8)], sems.at[0]),
        pltpu.make_async_copy(radius_hbm, radius, sems.at[1]),
        pltpu.make_async_copy(iblank_hbm, iblank, sems.at[2]),
        pltpu.make_async_copy(inv_xi_hbm, inv_xi, sems.at[3]),
    ]
    for copy in copies:
        copy.start()
    ext[:, 0:2] = xprev[...]
    ext[:, 10:12] = xnext[...]
    for c in range(10):
        v, x = divmod(4 * c, 8)
        lanes = slice(128 * c, 128 * (c + 1))
        t = jnp.concatenate([znext[:, lanes], jnp.zeros((112, 128), F32), zprev[:, lanes]], axis=0)
        zface[v, x : x + 4] = t.T.reshape(4, 32, 128)
    lane = lax.broadcasted_iota(jnp.int32, (32, 128), 1)
    row = lax.broadcasted_iota(jnp.int32, (32, 128), 0)
    has_low = eta == 1
    for copy in copies:
        copy.wait()

    def body(x, carry):
        rad = 0.04 * radius[x]
        keep = -iblank[x].astype(F32)
        fields = []
        for v in range(5):
            q = ext[v, x + 2]
            xp, xm = ext[v, x + 3], ext[v, x + 1]
            xpp, xmm = ext[v, x + 4], ext[v, x]
            face = yrec[v, x]
            lows = jnp.where(has_low, face, 0.0)
            highs = jnp.where(has_low, 0.0, face)
            l2, l1 = lows[6:7], lows[7:8]
            h1, h2 = highs[0:1], highs[1:2]
            yp = jnp.where(row == 31, h1, pltpu.roll(q, 31, 0))
            ypp = jnp.where(row == 31, h2, jnp.where(row == 30, h1, pltpu.roll(q, 30, 0)))
            ym = jnp.where(row == 0, l1, pltpu.roll(q, 1, 0))
            ymm = jnp.where(row == 0, l2, jnp.where(row == 1, l1, pltpu.roll(q, 2, 0)))
            z = zface[v, x]
            zp = pltpu.roll(jnp.where(lane == 0, z, q), 127, 1)
            zpp = pltpu.roll(jnp.where(lane < 2, z, q), 126, 1)
            zm = pltpu.roll(jnp.where(lane == 127, z, q), 1, 1)
            zmm = pltpu.roll(jnp.where(lane >= 126, z, q), 2, 1)
            flux = (
                (0.5 * speeds[0, v]) * (xp - xm)
                + (0.5 * speeds[1, v]) * (yp - ym)
                + (0.5 * speeds[2, v]) * (zp - zm)
            )
            far = (xpp + xmm) + (ypp + ymm) + (zpp + zmm)
            near = (xp + xm) + (yp + ym) + (zp + zm)
            diss = rad * (far - 4.0 * near + 18.0 * q)
            r = keep * (flux + diss)
            residual[v, x] = r
            fields.append(r)
        for v, value in enumerate(mixed(t_ref, 0, fields)):
            w0[v, x] = value
        return carry

    lax.fori_loop(0, 8, body, 0)
    for s, m in enumerate((m0, m1, m2, m3)):
        start = pl.multiple_of(8 * lax.rem(xi + s, 4), 8)
        m[:, 0:8] = w0[:, :, pl.ds(start, 8), :]
        m[:, 8] = jnp.concatenate([inv_xi[...], jnp.zeros((5, 8, 96), F32)], axis=2)


def residual_step(speeds, transforms, *arrays):
    return pl.pallas_call(
        residual_kernel,
        in_specs=[SMEM] * 2 + [HBM] * 4 + [VMEM] * 5,
        out_specs=[VMEM] * 5,
        out_shape=[shape(5, 8, 32, 128)] + [shape(5, 9, 8, 128)] * 4,
        scratch_shapes=[
            pltpu.VMEM((5, 12, 32, 128), F32),
            pltpu.VMEM((8, 32, 128), F32),
            pltpu.VMEM((8, 32, 128), jnp.int32),
            pltpu.VMEM((5, 8, 32), F32),
            pltpu.VMEM((5, 8, 32, 128), F32),
            pltpu.VMEM((5, 8, 32, 128), F32),
            pltpu.SemaphoreType.DMA((4,)),
        ],
        compiler_params=pltpu.CompilerParams(vmem_limit_bytes=16 << 20),
        name="residual",
    )(speeds, transforms, *arrays)


def xi_kernel(t_ref, r0, r1, r2, r3, b0, b1, b2, b3, field, inverse, work):
    xi, _, _, _ = position()
    for s, r in enumerate((r0, r1, r2, r3)):
        start = pl.multiple_of(8 * lax.rem(xi + 4 - s, 4), 8)
        field[:, pl.ds(start, 8)] = r[:, 0:8]
        inverse[:, pl.ds(start, 8), :] = r[:, 8]
    rows = lax.broadcasted_iota(jnp.int32, (256, 32), 0) // 8
    spread = (rows == lax.broadcasted_iota(jnp.int32, (256, 32), 1)).astype(F32).astype(BF16)
    cols = lax.broadcasted_iota(jnp.int32, (128, 256), 1) // 8
    widen = (cols == lax.broadcasted_iota(jnp.int32, (128, 256), 0)).astype(F32).astype(BF16)
    same = (
        lax.broadcasted_iota(jnp.int32, (256, 256), 0) % 8
        == lax.broadcasted_iota(jnp.int32, (256, 256), 1) % 8
    )
    for v in range(5):
        line = []
        for part in split(inverse[v]):
            wide = dot(part, widen, ((1,), (0,))).astype(BF16)
            full = dot(spread, wide, ((1,), (0,)))
            line.append(jnp.where(same, full, 0.0).astype(BF16))
        value = dot3(line, split(field[v].reshape(256, 128)))
        work[v] = value.reshape(32, 8, 128)

    def body(x, carry):
        for v, value in enumerate(mixed(t_ref, 1, [work[v, x] for v in range(5)])):
            field[v, x] = value
        return carry

    lax.fori_loop(0, 32, body, 0)
    for s, b in enumerate((b0, b1, b2, b3)):
        b[...] = field[:, pl.ds(8 * lax.rem(xi + s, 4), 8)]


def xi_step(transforms, parts):
    return pl.pallas_call(
        xi_kernel,
        in_specs=[SMEM] + [VMEM] * 4,
        out_specs=[VMEM] * 4,
        out_shape=[shape(5, 8, 8, 128)] * 4,
        scratch_shapes=[
            pltpu.VMEM((5, 32, 8, 128), F32),
            pltpu.VMEM((5, 32, 128), F32),
            pltpu.VMEM((5, 32, 8, 128), F32),
        ],
        compiler_params=pltpu.CompilerParams(vmem_limit_bytes=16 << 20),
        name="xi_lines",
    )(transforms, *parts)


def eta_kernel(t_ref, inv_eta, p0, p1, p2, p3, q0, q1, q2, q3, out, field, work):
    xi, eta, _, _ = position()
    for s, (p, q) in enumerate(zip((p0, p1, p2, p3), (q0, q1, q2, q3))):
        rows = 8 * lax.rem(xi + 4 - s, 4)
        field[:, :, pl.ds(pl.multiple_of(32 * eta + rows, 8), 8), :] = p[...]
        field[:, :, pl.ds(pl.multiple_of(32 * (1 - eta) + rows, 8), 8), :] = q[...]
    for v in range(5):
        wide = jnp.concatenate([field[v, x] for x in range(8)], axis=1)
        value = dot3(split(inv_eta[v]), split(wide))
        for x in range(8):
            work[v, x] = value[:, 128 * x : 128 * (x + 1)]


    def body(x, carry):
        for v, value in enumerate(mixed(t_ref, 2, [work[v, x] for v in range(5)])):
            out[v, x] = value
        return carry

    lax.fori_loop(0, 8, body, 0)


def eta_step(transforms, inv_eta, own, other):
    return pl.pallas_call(
        eta_kernel,
        in_specs=[SMEM] + [VMEM] * 9,
        out_specs=VMEM,
        out_shape=shape(5, 8, 32, 128),
        scratch_shapes=[pltpu.VMEM((5, 8, 64, 128), F32), pltpu.VMEM((5, 8, 32, 128), F32)],
        compiler_params=pltpu.CompilerParams(vmem_limit_bytes=16 << 20),
        name="eta_lines",
    )(transforms, inv_eta, *own, *other)


def pick_kernel(inv, *refs):
    _, eta, _, y = position()
    *outs, lines, sems = refs
    rows = pl.ds(pl.multiple_of(64 * eta, 64), 64)
    copies = [
        pltpu.make_async_copy(inv.at[v, rows], lines.at[v], sems.at[v]) for v in range(5)
    ]
    for copy in copies:
        copy.start()
    for v, copy in enumerate(copies):
        copy.wait()
        for s, first, count, g in zip(PICKED_STEP, PICKED_FIRST, PICKED_COUNT, outs):
            if first <= v < first + count:
                for z in range(NZC):
                    lanes = pl.multiple_of(512 * z + 128 * lax.rem(y + s, 4), 128)
                    g[z, v - first] = lines[v, :, pl.ds(lanes, 128)]


def pick(inv_zeta):
    return pl.pallas_call(
        pick_kernel,
        in_specs=[HBM],
        out_specs=[VMEM] * 4,
        out_shape=[shape(NZC, count, 64, 128) for count in PICKED_COUNT],
        scratch_shapes=[pltpu.VMEM((5, 64, 4096), F32), pltpu.SemaphoreType.DMA((5,))],
        compiler_params=pltpu.CompilerParams(vmem_limit_bytes=56 << 20),
        name="pick",
    )(inv_zeta)


def prepare_kernel(*refs):
    _, eta, _, _ = position()
    own_parts, other_parts, (high2, low2, high, low, lines) = refs[:4], refs[4:8], refs[8:]
    v = pl.program_id(0)

    def place(index, own, other):
        for half, part in ((eta, own), (1 - eta, other)):
            rows = pl.ds(pl.multiple_of(64 * half, 64), 64)
            for z in range(NZC):
                lines[PICKED_STEP[index] - 1, rows, 128 * z : 128 * (z + 1)] = part[z, 0]

    for index, (own, other) in enumerate(zip(own_parts, other_parts)):
        first, count = PICKED_FIRST[index], PICKED_COUNT[index]
        if count == 5:
            place(index, own, other)
        else:
            held = jnp.logical_and(v >= first, v < first + count)
            pl.when(held)(functools.partial(place, index, own, other))
    for z in range(NZC):
        rows = slice(128 * z, 128 * (z + 1))
        high2[0, rows], low2[0, rows] = split(lines[1, :, rows].T)
        for c in range(2):
            lanes = slice(128 * c, 128 * (c + 1))
            high[0, rows, lanes], low[0, rows, lanes] = split(lines[2 * c, :, rows].T)


def prepare(own_parts, other_parts):
    widths = (128, 128, 256, 256)

    def part(first, count):
        return pl.BlockSpec(
            (NZC, 1, 64, 128), lambda v: (0, jnp.clip(v - first, 0, count - 1), 0, 0)
        )

    parts = [part(*pair) for pair in zip(PICKED_FIRST, PICKED_COUNT)]
    return pl.pallas_call(
        prepare_kernel,
        grid=(5,),
        in_specs=parts * 2,
        out_specs=[pl.BlockSpec((1, 1024, w), lambda v: (v, 0, 0)) for w in widths],
        out_shape=[shape(5, 1024, w, dtype=BF16) for w in widths],
        scratch_shapes=[pltpu.VMEM((3, 128, 1024), F32)],
        compiler_params=pltpu.CompilerParams(vmem_limit_bytes=24 << 20),
        name="prepare",
    )(*own_parts, *other_parts)


def zeta_kernel(count, b_ref, *refs):
    b = split(jnp.concatenate([b_ref[z, 0].reshape(256, 128) for z in range(NZC)], axis=1))
    outs = list(refs[2 * count :])
    for high, low in zip(refs[0 : 2 * count : 2], refs[1 : 2 * count : 2]):
        value = dot3(b, (high[0], low[0]))
        for place in range(high.shape[2] // 128):
            lanes = slice(128 * place, 128 * (place + 1))
            outs.pop(0)[0] = value[:128, lanes]
            outs.pop(0)[0] = value[128:, lanes]


def zeta_step(gathered, *lines):
    widths = [array.shape[2] for array in lines]
    count = sum(widths) // 128
    return pl.pallas_call(
        functools.partial(zeta_kernel, len(lines) // 2),
        grid=(5,),
        in_specs=[pl.BlockSpec((NZC, 1, 8, 32, 128), lambda v: (0, v, 0, 0, 0))]
        + [pl.BlockSpec((1, 1024, w), lambda v: (v, 0, 0)) for w in widths],
        out_specs=[pl.BlockSpec((1, 128, 128), lambda v: (v, 0, 0))] * count,
        out_shape=[shape(5, 128, 128)] * count,
        compiler_params=pltpu.CompilerParams(vmem_limit_bytes=56 << 20),
        name="zeta_lines",
    )(gathered, *lines)


def own_kernel(b_ref, inv, out0, out1):
    _, _, _, y = position()
    b = split(jnp.concatenate([b_ref[z, 0].reshape(256, 128) for z in range(NZC)], axis=1))
    lanes = [pl.multiple_of(512 * z + 128 * y, 128) for z in range(NZC)]
    lines = jnp.concatenate([inv[0, :, pl.ds(lane, 128)] for lane in lanes], axis=1)
    value = dot3(b, split(lines), ((1,), (1,)))
    out0[0] = value[:128]
    out1[0] = value[128:]


def own_step(gathered, inv_zeta):
    return pl.pallas_call(
        own_kernel,
        grid=(5,),
        in_specs=[
            pl.BlockSpec((NZC, 1, 8, 32, 128), lambda v: (0, v, 0, 0, 0)),
            pl.BlockSpec((1, 128, 4096), lambda v: (v, 0, 0)),
        ],
        out_specs=[pl.BlockSpec((1, 128, 128), lambda v: (v, 0, 0))] * 2,
        out_shape=[shape(5, 128, 128)] * 2,
        compiler_params=pltpu.CompilerParams(vmem_limit_bytes=24 << 20),
        name="own_lines",
    )(gathered, inv_zeta)


def final_kernel(t_ref, state, own0, own1, low0, low1, high0, high1, out):
    for half, parts in enumerate(((own0, low0, high0), (own1, low1, high1))):

        def body(x, carry):
            rows = pl.ds(pl.multiple_of(32 * x, 32), 32)
            fields = [sum(part[v, rows] for part in parts) for v in range(5)]
            for v, value in enumerate(mixed(t_ref, 3, fields)):
                out[v, 4 * half + x] = state[v, 4 * half + x] + value
            return carry

        lax.fori_loop(0, 4, body, 0)


def final_step(transforms, state, parts):
    return pl.pallas_call(
        final_kernel,
        in_specs=[SMEM] + [VMEM] * 7,
        out_specs=VMEM,
        out_shape=shape(5, 8, 32, 128),
        compiler_params=pltpu.CompilerParams(vmem_limit_bytes=16 << 20),
        name="final",
    )(transforms, state, *parts)


def over_x(array, s):
    return lax.ppermute(array, "xi", [(i, (i + s) % 4) for i in range(4)])


def over_y(array, s):
    pairs = [(4 * z + y, 4 * z + (y + s) % 4) for z in range(NZC) for y in range(NYC)]
    return lax.ppermute(array, "zeta", pairs)


def over_core(array):
    return lax.ppermute(array, "eta", [(0, 1), (1, 0)])


def shift_line(array, axis, s):
    size = lax.axis_size(axis)
    pairs = [(i, i + s) for i in range(size) if 0 <= i + s < size]
    return lax.ppermute(array, axis, pairs)


def after(array, *first):
    return lax.optimization_barrier((array, *first))[0]


def local(state, radius, iblank, speeds, transforms, inv_xi, inv_eta, inv_zeta):
    xlo, xhi, yface, zlo, zhi = faces(state)
    halos = [
        shift_line(xhi, "xi", 1),
        shift_line(xlo, "xi", -1),
        over_core(yface),
        shift_line(zhi, "zeta", 1),
        shift_line(zlo, "zeta", -1),
    ]
    picked = pick(inv_zeta)
    halos[0] = after(halos[0], picked[0])
    residual, m0, m1, m2, m3 = residual_step(
        speeds, transforms, state, radius, iblank, inv_xi, *halos
    )
    parts = [m0] + [over_x(m, s + 1) for s, m in enumerate((m1, m2, m3))]
    sent = [over_y(after(picked[0], m0), PICKED_STEP[0])]
    b0, b1, b2, b3 = xi_step(transforms, parts)
    own = [b0] + [over_x(b, s + 1) for s, b in enumerate((b1, b2, b3))]
    other = [over_core(p) for p in own]
    own[0] = after(own[0], *sent)
    work = eta_step(transforms, inv_eta, own, other)

    columns = [[4 * z + y for z in range(NZC)] for y in range(NYC)]
    gathered = lax.all_gather(work, "zeta", axis_index_groups=columns)
    sent += [over_y(after(picked[i], work), PICKED_STEP[i]) for i in range(1, 4)]
    swapped = [over_core(after(part, work)) for part in sent]
    high2, low2, high, low = prepare(sent, swapped)

    far0, far1 = zeta_step(gathered, high2, low2)
    far0, far1 = over_y(far0, 1), over_y(far1, -1)
    down0, down1, up0, up1 = zeta_step(gathered, high, low)
    own0, own1 = own_step(gathered, after(inv_zeta, down0, up1))
    up1, down0 = over_y(up1, 1), over_y(down0, -1)
    up0, down1 = over_y(up0 + far0, 1), over_y(down1 + far1, -1)
    advanced = final_step(transforms, state, (own0, own1, up0, up1, down0, down1))
    return residual, advanced


def solution(mesh):
    placed = (
        P(None, "xi", "eta", "zeta"),
        P("xi", "eta", "zeta"),
        P("xi", "eta", "zeta"),
        P(),
        P(),
        P(None, "xi", None),
        P(None, "eta", None),
        P(None, "zeta", None),
    )
    return jax.shard_map(
        local,
        mesh=mesh,
        in_specs=placed,
        out_specs=(P(None, "xi", "eta", "zeta"), P(None, "xi", "eta", "zeta")),
        check_vma=False,
    )
```

```python
import functools

import jax
import jax.numpy as jnp
from jax import lax
from jax.experimental import pallas as pl
from jax.experimental.pallas import tpu as pltpu
from jax.sharding import PartitionSpec as P

F32 = jnp.float32
BF16 = jnp.bfloat16
SMEM = pl.BlockSpec(memory_space=pltpu.SMEM)
HBM = pl.BlockSpec(memory_space=pltpu.HBM)
VMEM = pl.BlockSpec()
NZC, NYC = 8, 4
PICKED_STEP = (2, 2, 1, 3)
PICKED_FIRST = (0, 3, 0, 0)
PICKED_COUNT = (3, 2, 5, 5)


def position():
    xi, eta, zeta = (lax.axis_index(name) for name in ("xi", "eta", "zeta"))
    return xi, eta, lax.div(zeta, 4), lax.rem(zeta, 4)


def shape(*dims, dtype=F32):
    return jax.ShapeDtypeStruct(dims, dtype)


def split(x):
    high = x.astype(BF16)
    low = (x - high.astype(F32)).astype(BF16)
    return high, low


def dot(a, b, dims):
    return lax.dot_general(a, b, (dims, ((), ())), preferred_element_type=F32)


def dot3(a, b, dims=((1,), (0,))):
    a_high, a_low = a
    b_high, b_low = b
    return dot(a_high, b_high, dims) + dot(a_high, b_low, dims) + dot(a_low, b_high, dims)


def mixed(t_ref, which, fields):
    out = []
    for a in range(5):
        total = t_ref[which, a, 0] * fields[0]
        for b in range(1, 5):
            total = total + t_ref[which, a, b] * fields[b]
        out.append(total)
    return out


def faces_kernel(state, xlo, xhi, yface, zlo, zhi):
    _, eta, _, _ = position()
    xlo[...] = state[:, 0:2]
    xhi[...] = state[:, 6:8]
    start = pl.multiple_of(24 * (1 - eta), 8)
    yface[...] = state[:, :, pl.ds(start, 8), :]
    for c in range(10):
        v, x = divmod(4 * c, 8)
        t = state[v, x : x + 4].reshape(128, 128).T
        zlo[:, 128 * c : 128 * (c + 1)] = t[0:8]
        zhi[:, 128 * c : 128 * (c + 1)] = t[120:128]


def faces(state):
    return pl.pallas_call(
        faces_kernel,
        in_specs=[VMEM],
        out_specs=[VMEM] * 5,
        out_shape=[
            shape(5, 2, 32, 128),
            shape(5, 2, 32, 128),
            shape(5, 8, 8, 128),
            shape(8, 1280),
            shape(8, 1280),
        ],
        name="faces",
    )(state)


def residual_kernel(
    speeds, t_ref, state, radius_hbm, iblank_hbm, inv_xi_hbm, xprev, xnext, yrec, zprev, znext,
    residual, m0, m1, m2, m3, ext, radius, iblank, inv_xi, zface, w0, sems,
):
    xi, eta, _, _ = position()
    copies = [
        pltpu.make_async_copy(state, ext.at[:, pl.ds(2, 8)], sems.at[0]),
        pltpu.make_async_copy(radius_hbm, radius, sems.at[1]),
        pltpu.make_async_copy(iblank_hbm, iblank, sems.at[2]),
        pltpu.make_async_copy(inv_xi_hbm, inv_xi, sems.at[3]),
    ]
    for copy in copies:
        copy.start()
    ext[:, 0:2] = xprev[...]
    ext[:, 10:12] = xnext[...]
    for c in range(10):
        v, x = divmod(4 * c, 8)
        lanes = slice(128 * c, 128 * (c + 1))
        t = jnp.concatenate([znext[:, lanes], jnp.zeros((112, 128), F32), zprev[:, lanes]], axis=0)
        zface[v, x : x + 4] = t.T.reshape(4, 32, 128)
    lane = lax.broadcasted_iota(jnp.int32, (32, 128), 1)
    row = lax.broadcasted_iota(jnp.int32, (32, 128), 0)
    has_low = eta == 1
    for copy in copies:
        copy.wait()

    def body(x, carry):
        rad = 0.04 * radius[x]
        keep = -iblank[x].astype(F32)
        fields = []
        for v in range(5):
            q = ext[v, x + 2]
            xp, xm = ext[v, x + 3], ext[v, x + 1]
            xpp, xmm = ext[v, x + 4], ext[v, x]
            face = yrec[v, x]
            lows = jnp.where(has_low, face, 0.0)
            highs = jnp.where(has_low, 0.0, face)
            l2, l1 = lows[6:7], lows[7:8]
            h1, h2 = highs[0:1], highs[1:2]
            yp = jnp.where(row == 31, h1, pltpu.roll(q, 31, 0))
            ypp = jnp.where(row == 31, h2, jnp.where(row == 30, h1, pltpu.roll(q, 30, 0)))
            ym = jnp.where(row == 0, l1, pltpu.roll(q, 1, 0))
            ymm = jnp.where(row == 0, l2, jnp.where(row == 1, l1, pltpu.roll(q, 2, 0)))
            z = zface[v, x]
            zp = pltpu.roll(jnp.where(lane == 0, z, q), 127, 1)
            zpp = pltpu.roll(jnp.where(lane < 2, z, q), 126, 1)
            zm = pltpu.roll(jnp.where(lane == 127, z, q), 1, 1)
            zmm = pltpu.roll(jnp.where(lane >= 126, z, q), 2, 1)
            flux = (
                (0.5 * speeds[0, v]) * (xp - xm)
                + (0.5 * speeds[1, v]) * (yp - ym)
                + (0.5 * speeds[2, v]) * (zp - zm)
            )
            far = (xpp + xmm) + (ypp + ymm) + (zpp + zmm)
            near = (xp + xm) + (yp + ym) + (zp + zm)
            diss = rad * (far - 4.0 * near + 18.0 * q)
            r = keep * (flux + diss)
            residual[v, x] = r
            fields.append(r)
        for v, value in enumerate(mixed(t_ref, 0, fields)):
            w0[v, x] = value
        return carry

    lax.fori_loop(0, 8, body, 0)
    for s, m in enumerate((m0, m1, m2, m3)):
        start = pl.multiple_of(8 * lax.rem(xi + s, 4), 8)
        m[:, 0:8] = w0[:, :, pl.ds(start, 8), :]
        m[:, 8] = jnp.concatenate([inv_xi[...], jnp.zeros((5, 8, 96), F32)], axis=2)


def residual_step(speeds, transforms, *arrays):
    return pl.pallas_call(
        residual_kernel,
        in_specs=[SMEM] * 2 + [HBM] * 4 + [VMEM] * 5,
        out_specs=[VMEM] * 5,
        out_shape=[shape(5, 8, 32, 128)] + [shape(5, 9, 8, 128)] * 4,
        scratch_shapes=[
            pltpu.VMEM((5, 12, 32, 128), F32),
            pltpu.VMEM((8, 32, 128), F32),
            pltpu.VMEM((8, 32, 128), jnp.int32),
            pltpu.VMEM((5, 8, 32), F32),
            pltpu.VMEM((5, 8, 32, 128), F32),
            pltpu.VMEM((5, 8, 32, 128), F32),
            pltpu.SemaphoreType.DMA((4,)),
        ],
        compiler_params=pltpu.CompilerParams(vmem_limit_bytes=16 << 20),
        name="residual",
    )(speeds, transforms, *arrays)


def xi_kernel(t_ref, r0, r1, r2, r3, b0, b1, b2, b3, field, inverse, work):
    xi, _, _, _ = position()
    for s, r in enumerate((r0, r1, r2, r3)):
        start = pl.multiple_of(8 * lax.rem(xi + 4 - s, 4), 8)
        field[:, pl.ds(start, 8)] = r[:, 0:8]
        inverse[:, pl.ds(start, 8), :] = r[:, 8]
    rows = lax.broadcasted_iota(jnp.int32, (256, 32), 0) // 8
    spread = (rows == lax.broadcasted_iota(jnp.int32, (256, 32), 1)).astype(F32).astype(BF16)
    cols = lax.broadcasted_iota(jnp.int32, (128, 256), 1) // 8
    widen = (cols == lax.broadcasted_iota(jnp.int32, (128, 256), 0)).astype(F32).astype(BF16)
    same = (
        lax.broadcasted_iota(jnp.int32, (256, 256), 0) % 8
        == lax.broadcasted_iota(jnp.int32, (256, 256), 1) % 8
    )
    for v in range(5):
        line = []
        for part in split(inverse[v]):
            wide = dot(part, widen, ((1,), (0,))).astype(BF16)
            full = dot(spread, wide, ((1,), (0,)))
            line.append(jnp.where(same, full, 0.0).astype(BF16))
        value = dot3(line, split(field[v].reshape(256, 128)))
        work[v] = value.reshape(32, 8, 128)

    def body(x, carry):
        for v, value in enumerate(mixed(t_ref, 1, [work[v, x] for v in range(5)])):
            field[v, x] = value
        return carry

    lax.fori_loop(0, 32, body, 0)
    for s, b in enumerate((b0, b1, b2, b3)):
        b[...] = field[:, pl.ds(8 * lax.rem(xi + s, 4), 8)]


def xi_step(transforms, parts):
    return pl.pallas_call(
        xi_kernel,
        in_specs=[SMEM] + [VMEM] * 4,
        out_specs=[VMEM] * 4,
        out_shape=[shape(5, 8, 8, 128)] * 4,
        scratch_shapes=[
            pltpu.VMEM((5, 32, 8, 128), F32),
            pltpu.VMEM((5, 32, 128), F32),
            pltpu.VMEM((5, 32, 8, 128), F32),
        ],
        compiler_params=pltpu.CompilerParams(vmem_limit_bytes=16 << 20),
        name="xi_lines",
    )(transforms, *parts)


def eta_kernel(t_ref, inv_eta, p0, p1, p2, p3, q0, q1, q2, q3, out, field, work):
    xi, eta, _, _ = position()
    for s, (p, q) in enumerate(zip((p0, p1, p2, p3), (q0, q1, q2, q3))):
        rows = 8 * lax.rem(xi + 4 - s, 4)
        field[:, :, pl.ds(pl.multiple_of(32 * eta + rows, 8), 8), :] = p[...]
        field[:, :, pl.ds(pl.multiple_of(32 * (1 - eta) + rows, 8), 8), :] = q[...]
    for v in range(5):
        wide = jnp.concatenate([field[v, x] for x in range(8)], axis=1)
        value = dot3(split(inv_eta[v]), split(wide))
        for x in range(8):
            work[v, x] = value[:, 128 * x : 128 * (x + 1)]


    def body(x, carry):
        for v, value in enumerate(mixed(t_ref, 2, [work[v, x] for v in range(5)])):
            out[v, x] = value
        return carry

    lax.fori_loop(0, 8, body, 0)


def eta_step(transforms, inv_eta, own, other):
    return pl.pallas_call(
        eta_kernel,
        in_specs=[SMEM] + [VMEM] * 9,
        out_specs=VMEM,
        out_shape=shape(5, 8, 32, 128),
        scratch_shapes=[pltpu.VMEM((5, 8, 64, 128), F32), pltpu.VMEM((5, 8, 32, 128), F32)],
        compiler_params=pltpu.CompilerParams(vmem_limit_bytes=16 << 20),
        name="eta_lines",
    )(transforms, inv_eta, *own, *other)


def pick_kernel(inv, *refs):
    _, eta, _, y = position()
    *outs, lines, sems = refs
    rows = pl.ds(pl.multiple_of(64 * eta, 64), 64)
    copies = [
        pltpu.make_async_copy(inv.at[v, rows], lines.at[v], sems.at[v]) for v in range(5)
    ]
    for copy in copies:
        copy.start()
    for v, copy in enumerate(copies):
        copy.wait()
        for s, first, count, g in zip(PICKED_STEP, PICKED_FIRST, PICKED_COUNT, outs):
            if first <= v < first + count:
                for z in range(NZC):
                    lanes = pl.multiple_of(512 * z + 128 * lax.rem(y + s, 4), 128)
                    g[z, v - first] = lines[v, :, pl.ds(lanes, 128)]


def pick(inv_zeta):
    return pl.pallas_call(
        pick_kernel,
        in_specs=[HBM],
        out_specs=[VMEM] * 4,
        out_shape=[shape(NZC, count, 64, 128) for count in PICKED_COUNT],
        scratch_shapes=[pltpu.VMEM((5, 64, 4096), F32), pltpu.SemaphoreType.DMA((5,))],
        compiler_params=pltpu.CompilerParams(vmem_limit_bytes=56 << 20),
        name="pick",
    )(inv_zeta)


def prepare_kernel(*refs):
    _, eta, _, _ = position()
    own_parts, other_parts, (high2, low2, high, low, lines) = refs[:4], refs[4:8], refs[8:]
    v = pl.program_id(0)

    def place(index, own, other):
        for half, part in ((eta, own), (1 - eta, other)):
            rows = pl.ds(pl.multiple_of(64 * half, 64), 64)
            for z in range(NZC):
                lines[PICKED_STEP[index] - 1, rows, 128 * z : 128 * (z + 1)] = part[z, 0]

    for index, (own, other) in enumerate(zip(own_parts, other_parts)):
        first, count = PICKED_FIRST[index], PICKED_COUNT[index]
        if count == 5:
            place(index, own, other)
        else:
            held = jnp.logical_and(v >= first, v < first + count)
            pl.when(held)(functools.partial(place, index, own, other))
    for z in range(NZC):
        rows = slice(128 * z, 128 * (z + 1))
        high2[0, rows], low2[0, rows] = split(lines[1, :, rows].T)
        for c in range(2):
            lanes = slice(128 * c, 128 * (c + 1))
            high[0, rows, lanes], low[0, rows, lanes] = split(lines[2 * c, :, rows].T)


def prepare(own_parts, other_parts):
    widths = (128, 128, 256, 256)

    def part(first, count):
        return pl.BlockSpec(
            (NZC, 1, 64, 128), lambda v: (0, jnp.clip(v - first, 0, count - 1), 0, 0)
        )

    parts = [part(*pair) for pair in zip(PICKED_FIRST, PICKED_COUNT)]
    return pl.pallas_call(
        prepare_kernel,
        grid=(5,),
        in_specs=parts * 2,
        out_specs=[pl.BlockSpec((1, 1024, w), lambda v: (v, 0, 0)) for w in widths],
        out_shape=[shape(5, 1024, w, dtype=BF16) for w in widths],
        scratch_shapes=[pltpu.VMEM((3, 128, 1024), F32)],
        compiler_params=pltpu.CompilerParams(vmem_limit_bytes=24 << 20),
        name="prepare",
    )(*own_parts, *other_parts)


def zeta_kernel(count, b_ref, *refs):
    b = split(jnp.concatenate([b_ref[z, 0].reshape(256, 128) for z in range(NZC)], axis=1))
    outs = list(refs[2 * count :])
    for high, low in zip(refs[0 : 2 * count : 2], refs[1 : 2 * count : 2]):
        value = dot3(b, (high[0], low[0]))
        for place in range(high.shape[2] // 128):
            lanes = slice(128 * place, 128 * (place + 1))
            outs.pop(0)[0] = value[:128, lanes]
            outs.pop(0)[0] = value[128:, lanes]


def zeta_step(gathered, *lines, limit):
    widths = [array.shape[2] for array in lines]
    count = sum(widths) // 128
    return pl.pallas_call(
        functools.partial(zeta_kernel, len(lines) // 2),
        grid=(5,),
        in_specs=[pl.BlockSpec((NZC, 1, 8, 32, 128), lambda v: (0, v, 0, 0, 0))]
        + [pl.BlockSpec((1, 1024, w), lambda v: (v, 0, 0)) for w in widths],
        out_specs=[pl.BlockSpec((1, 128, 128), lambda v: (v, 0, 0))] * count,
        out_shape=[shape(5, 128, 128)] * count,
        compiler_params=pltpu.CompilerParams(vmem_limit_bytes=limit << 20),
        name="zeta_lines",
    )(gathered, *lines)


def own_kernel(b_ref, inv, out0, out1):
    _, _, _, y = position()
    b = split(jnp.concatenate([b_ref[z, 0].reshape(256, 128) for z in range(NZC)], axis=1))
    lanes = [pl.multiple_of(512 * z + 128 * y, 128) for z in range(NZC)]
    lines = jnp.concatenate([inv[0, :, pl.ds(lane, 128)] for lane in lanes], axis=1)
    value = dot3(b, split(lines), ((1,), (1,)))
    out0[0] = value[:128]
    out1[0] = value[128:]


def own_step(gathered, inv_zeta):
    return pl.pallas_call(
        own_kernel,
        grid=(5,),
        in_specs=[
            pl.BlockSpec((NZC, 1, 8, 32, 128), lambda v: (0, v, 0, 0, 0)),
            pl.BlockSpec((1, 128, 4096), lambda v: (v, 0, 0)),
        ],
        out_specs=[pl.BlockSpec((1, 128, 128), lambda v: (v, 0, 0))] * 2,
        out_shape=[shape(5, 128, 128)] * 2,
        compiler_params=pltpu.CompilerParams(vmem_limit_bytes=24 << 20),
        name="own_lines",
    )(gathered, inv_zeta)


def final_kernel(t_ref, state, own0, own1, low0, low1, high0, high1, out):
    for half, parts in enumerate(((own0, low0, high0), (own1, low1, high1))):

        def body(x, carry):
            rows = pl.ds(pl.multiple_of(32 * x, 32), 32)
            fields = [sum(part[v, rows] for part in parts) for v in range(5)]
            for v, value in enumerate(mixed(t_ref, 3, fields)):
                out[v, 4 * half + x] = state[v, 4 * half + x] + value
            return carry

        lax.fori_loop(0, 4, body, 0)


def final_step(transforms, state, parts):
    return pl.pallas_call(
        final_kernel,
        in_specs=[SMEM] + [VMEM] * 7,
        out_specs=VMEM,
        out_shape=shape(5, 8, 32, 128),
        compiler_params=pltpu.CompilerParams(vmem_limit_bytes=16 << 20),
        name="final",
    )(transforms, state, *parts)


def over_x(array, s):
    return lax.ppermute(array, "xi", [(i, (i + s) % 4) for i in range(4)])


def over_y(array, s):
    pairs = [(4 * z + y, 4 * z + (y + s) % 4) for z in range(NZC) for y in range(NYC)]
    return lax.ppermute(array, "zeta", pairs)


def over_core(array):
    return lax.ppermute(array, "eta", [(0, 1), (1, 0)])


def shift_line(array, axis, s):
    size = lax.axis_size(axis)
    pairs = [(i, i + s) for i in range(size) if 0 <= i + s < size]
    return lax.ppermute(array, axis, pairs)


def after(array, *first):
    return lax.optimization_barrier((array, *first))[0]


def local(state, radius, iblank, speeds, transforms, inv_xi, inv_eta, inv_zeta):
    xlo, xhi, yface, zlo, zhi = faces(state)
    halos = [
        shift_line(xhi, "xi", 1),
        shift_line(xlo, "xi", -1),
        over_core(yface),
        shift_line(zhi, "zeta", 1),
        shift_line(zlo, "zeta", -1),
    ]
    picked = pick(inv_zeta)
    halos[0] = after(halos[0], picked[0])
    residual, m0, m1, m2, m3 = residual_step(
        speeds, transforms, state, radius, iblank, inv_xi, *halos
    )
    parts = [m0] + [over_x(m, s + 1) for s, m in enumerate((m1, m2, m3))]
    sent = [over_y(after(picked[0], m0), PICKED_STEP[0])]
    b0, b1, b2, b3 = xi_step(transforms, parts)
    own = [b0] + [over_x(b, s + 1) for s, b in enumerate((b1, b2, b3))]
    other = [over_core(p) for p in own]
    own[0] = after(own[0], *sent)
    work = eta_step(transforms, inv_eta, own, other)

    columns = [[4 * z + y for z in range(NZC)] for y in range(NYC)]
    gathered = lax.all_gather(work, "zeta", axis_index_groups=columns)
    sent += [over_y(after(picked[i], work), PICKED_STEP[i]) for i in range(1, 4)]
    swapped = [over_core(after(part, work)) for part in sent]
    high2, low2, high, low = prepare(sent, swapped)

    far0, far1 = zeta_step(gathered, high2, low2, limit=56)
    far0, far1 = over_y(far0, 1), over_y(far1, -1)
    down0, down1, up0, up1 = zeta_step(gathered, high, low, limit=24)
    own0, own1 = own_step(gathered, after(inv_zeta, down0, up1))
    up1, down0 = over_y(up1, 1), over_y(down0, -1)
    up0, down1 = over_y(up0 + far0, 1), over_y(down1 + far1, -1)
    advanced = final_step(transforms, state, (own0, own1, up0, up1, down0, down1))
    return residual, advanced


def solution(mesh):
    placed = (
        P(None, "xi", "eta", "zeta"),
        P("xi", "eta", "zeta"),
        P("xi", "eta", "zeta"),
        P(),
        P(),
        P(None, "xi", None),
        P(None, "eta", None),
        P(None, "zeta", None),
    )
    return jax.shard_map(
        local,
        mesh=mesh,
        in_specs=placed,
        out_specs=(P(None, "xi", "eta", "zeta"), P(None, "xi", "eta", "zeta")),
        check_vma=False,
    )
```

```python
import functools

import jax
import jax.numpy as jnp
from jax import lax
from jax.experimental import pallas as pl
from jax.experimental.pallas import tpu as pltpu
from jax.sharding import PartitionSpec as P

F32 = jnp.float32
BF16 = jnp.bfloat16
SMEM = pl.BlockSpec(memory_space=pltpu.SMEM)
HBM = pl.BlockSpec(memory_space=pltpu.HBM)
VMEM = pl.BlockSpec()
NZC, NYC = 8, 4
PICKED_STEP = (2, 2, 1, 3)
PICKED_FIRST = (0, 3, 0, 0)
PICKED_COUNT = (3, 2, 5, 5)


def position():
    xi, eta, zeta = (lax.axis_index(name) for name in ("xi", "eta", "zeta"))
    return xi, eta, lax.div(zeta, 4), lax.rem(zeta, 4)


def shape(*dims, dtype=F32):
    return jax.ShapeDtypeStruct(dims, dtype)


def split(x):
    high = x.astype(BF16)
    low = (x - high.astype(F32)).astype(BF16)
    return high, low


def dot(a, b, dims):
    return lax.dot_general(a, b, (dims, ((), ())), preferred_element_type=F32)


def dot3(a, b, dims=((1,), (0,))):
    a_high, a_low = a
    b_high, b_low = b
    return dot(a_high, b_high, dims) + dot(a_high, b_low, dims) + dot(a_low, b_high, dims)


def mixed(t_ref, which, fields):
    out = []
    for a in range(5):
        total = t_ref[which, a, 0] * fields[0]
        for b in range(1, 5):
            total = total + t_ref[which, a, b] * fields[b]
        out.append(total)
    return out


def faces_kernel(state, xlo, xhi, yface, zlo, zhi):
    _, eta, _, _ = position()
    xlo[...] = state[:, 0:2]
    xhi[...] = state[:, 6:8]
    start = pl.multiple_of(24 * (1 - eta), 8)
    yface[...] = state[:, :, pl.ds(start, 8), :]
    for c in range(10):
        v, x = divmod(4 * c, 8)
        t = state[v, x : x + 4].reshape(128, 128).T
        zlo[:, 128 * c : 128 * (c + 1)] = t[0:8]
        zhi[:, 128 * c : 128 * (c + 1)] = t[120:128]


def faces(state):
    return pl.pallas_call(
        faces_kernel,
        in_specs=[VMEM],
        out_specs=[VMEM] * 5,
        out_shape=[
            shape(5, 2, 32, 128),
            shape(5, 2, 32, 128),
            shape(5, 8, 8, 128),
            shape(8, 1280),
            shape(8, 1280),
        ],
        name="faces",
    )(state)


def residual_kernel(
    speeds, t_ref, state, radius_hbm, iblank_hbm, inv_xi_hbm, xprev, xnext, yrec, zprev, znext,
    residual, m0, m1, m2, m3, ext, radius, iblank, inv_xi, zface, w0, sems,
):
    xi, eta, _, _ = position()
    copies = [
        pltpu.make_async_copy(state, ext.at[:, pl.ds(2, 8)], sems.at[0]),
        pltpu.make_async_copy(radius_hbm, radius, sems.at[1]),
        pltpu.make_async_copy(iblank_hbm, iblank, sems.at[2]),
        pltpu.make_async_copy(inv_xi_hbm, inv_xi, sems.at[3]),
    ]
    for copy in copies:
        copy.start()
    ext[:, 0:2] = xprev[...]
    ext[:, 10:12] = xnext[...]
    for c in range(10):
        v, x = divmod(4 * c, 8)
        lanes = slice(128 * c, 128 * (c + 1))
        t = jnp.concatenate([znext[:, lanes], jnp.zeros((112, 128), F32), zprev[:, lanes]], axis=0)
        zface[v, x : x + 4] = t.T.reshape(4, 32, 128)
    lane = lax.broadcasted_iota(jnp.int32, (32, 128), 1)
    row = lax.broadcasted_iota(jnp.int32, (32, 128), 0)
    has_low = eta == 1
    for copy in copies:
        copy.wait()

    def body(x, carry):
        rad = 0.04 * radius[x]
        keep = -iblank[x].astype(F32)
        fields = []
        for v in range(5):
            q = ext[v, x + 2]
            xp, xm = ext[v, x + 3], ext[v, x + 1]
            xpp, xmm = ext[v, x + 4], ext[v, x]
            face = yrec[v, x]
            lows = jnp.where(has_low, face, 0.0)
            highs = jnp.where(has_low, 0.0, face)
            l2, l1 = lows[6:7], lows[7:8]
            h1, h2 = highs[0:1], highs[1:2]
            yp = jnp.where(row == 31, h1, pltpu.roll(q, 31, 0))
            ypp = jnp.where(row == 31, h2, jnp.where(row == 30, h1, pltpu.roll(q, 30, 0)))
            ym = jnp.where(row == 0, l1, pltpu.roll(q, 1, 0))
            ymm = jnp.where(row == 0, l2, jnp.where(row == 1, l1, pltpu.roll(q, 2, 0)))
            z = zface[v, x]
            zp = pltpu.roll(jnp.where(lane == 0, z, q), 127, 1)
            zpp = pltpu.roll(jnp.where(lane < 2, z, q), 126, 1)
            zm = pltpu.roll(jnp.where(lane == 127, z, q), 1, 1)
            zmm = pltpu.roll(jnp.where(lane >= 126, z, q), 2, 1)
            flux = (
                (0.5 * speeds[0, v]) * (xp - xm)
                + (0.5 * speeds[1, v]) * (yp - ym)
                + (0.5 * speeds[2, v]) * (zp - zm)
            )
            far = (xpp + xmm) + (ypp + ymm) + (zpp + zmm)
            near = (xp + xm) + (yp + ym) + (zp + zm)
            diss = rad * (far - 4.0 * near + 18.0 * q)
            r = keep * (flux + diss)
            residual[v, x] = r
            fields.append(r)
        for v, value in enumerate(mixed(t_ref, 0, fields)):
            w0[v, x] = value
        return carry

    lax.fori_loop(0, 8, body, 0)
    for s, m in enumerate((m0, m1, m2, m3)):
        start = pl.multiple_of(8 * lax.rem(xi + s, 4), 8)
        m[:, 0:8] = w0[:, :, pl.ds(start, 8), :]
        m[:, 8] = jnp.concatenate([inv_xi[...], jnp.zeros((5, 8, 96), F32)], axis=2)


def residual_step(speeds, transforms, *arrays):
    return pl.pallas_call(
        residual_kernel,
        in_specs=[SMEM] * 2 + [HBM] * 4 + [VMEM] * 5,
        out_specs=[VMEM] * 5,
        out_shape=[shape(5, 8, 32, 128)] + [shape(5, 9, 8, 128)] * 4,
        scratch_shapes=[
            pltpu.VMEM((5, 12, 32, 128), F32),
            pltpu.VMEM((8, 32, 128), F32),
            pltpu.VMEM((8, 32, 128), jnp.int32),
            pltpu.VMEM((5, 8, 32), F32),
            pltpu.VMEM((5, 8, 32, 128), F32),
            pltpu.VMEM((5, 8, 32, 128), F32),
            pltpu.SemaphoreType.DMA((4,)),
        ],
        compiler_params=pltpu.CompilerParams(vmem_limit_bytes=16 << 20),
        name="residual",
    )(speeds, transforms, *arrays)


def xi_kernel(t_ref, r0, r1, r2, r3, b0, b1, b2, b3, field, inverse, work):
    xi, _, _, _ = position()
    for s, r in enumerate((r0, r1, r2, r3)):
        start = pl.multiple_of(8 * lax.rem(xi + 4 - s, 4), 8)
        field[:, pl.ds(start, 8)] = r[:, 0:8]
        inverse[:, pl.ds(start, 8), :] = r[:, 8]
    rows = lax.broadcasted_iota(jnp.int32, (256, 32), 0) // 8
    spread = (rows == lax.broadcasted_iota(jnp.int32, (256, 32), 1)).astype(F32).astype(BF16)
    cols = lax.broadcasted_iota(jnp.int32, (128, 256), 1) // 8
    widen = (cols == lax.broadcasted_iota(jnp.int32, (128, 256), 0)).astype(F32).astype(BF16)
    same = (
        lax.broadcasted_iota(jnp.int32, (256, 256), 0) % 8
        == lax.broadcasted_iota(jnp.int32, (256, 256), 1) % 8
    )
    for v in range(5):
        line = []
        for part in split(inverse[v]):
            wide = dot(part, widen, ((1,), (0,))).astype(BF16)
            full = dot(spread, wide, ((1,), (0,)))
            line.append(jnp.where(same, full, 0.0).astype(BF16))
        value = dot3(line, split(field[v].reshape(256, 128)))
        work[v] = value.reshape(32, 8, 128)

    def body(x, carry):
        for v, value in enumerate(mixed(t_ref, 1, [work[v, x] for v in range(5)])):
            field[v, x] = value
        return carry

    lax.fori_loop(0, 32, body, 0)
    for s, b in enumerate((b0, b1, b2, b3)):
        b[...] = field[:, pl.ds(8 * lax.rem(xi + s, 4), 8)]


def xi_step(transforms, parts):
    return pl.pallas_call(
        xi_kernel,
        in_specs=[SMEM] + [VMEM] * 4,
        out_specs=[VMEM] * 4,
        out_shape=[shape(5, 8, 8, 128)] * 4,
        scratch_shapes=[
            pltpu.VMEM((5, 32, 8, 128), F32),
            pltpu.VMEM((5, 32, 128), F32),
            pltpu.VMEM((5, 32, 8, 128), F32),
        ],
        compiler_params=pltpu.CompilerParams(vmem_limit_bytes=16 << 20),
        name="xi_lines",
    )(transforms, *parts)


def eta_kernel(t_ref, inv_eta, p0, p1, p2, p3, q0, q1, q2, q3, out, field, work):
    xi, eta, _, _ = position()
    for s, (p, q) in enumerate(zip((p0, p1, p2, p3), (q0, q1, q2, q3))):
        rows = 8 * lax.rem(xi + 4 - s, 4)
        field[:, :, pl.ds(pl.multiple_of(32 * eta + rows, 8), 8), :] = p[...]
        field[:, :, pl.ds(pl.multiple_of(32 * (1 - eta) + rows, 8), 8), :] = q[...]
    for v in range(5):
        wide = jnp.concatenate([field[v, x] for x in range(8)], axis=1)
        value = dot3(split(inv_eta[v]), split(wide))
        for x in range(8):
            work[v, x] = value[:, 128 * x : 128 * (x + 1)]


    def body(x, carry):
        for v, value in enumerate(mixed(t_ref, 2, [work[v, x] for v in range(5)])):
            out[v, x] = value
        return carry

    lax.fori_loop(0, 8, body, 0)


def eta_step(transforms, inv_eta, own, other):
    return pl.pallas_call(
        eta_kernel,
        in_specs=[SMEM] + [VMEM] * 9,
        out_specs=VMEM,
        out_shape=shape(5, 8, 32, 128),
        scratch_shapes=[pltpu.VMEM((5, 8, 64, 128), F32), pltpu.VMEM((5, 8, 32, 128), F32)],
        compiler_params=pltpu.CompilerParams(vmem_limit_bytes=16 << 20),
        name="eta_lines",
    )(transforms, inv_eta, *own, *other)


def pick_kernel(inv, *refs):
    _, eta, _, y = position()
    *outs, lines, sems = refs
    rows = pl.ds(pl.multiple_of(64 * eta, 64), 64)
    copies = [
        pltpu.make_async_copy(inv.at[v, rows], lines.at[v], sems.at[v]) for v in range(5)
    ]
    for copy in copies:
        copy.start()
    for v, copy in enumerate(copies):
        copy.wait()
        for s, first, count, g in zip(PICKED_STEP, PICKED_FIRST, PICKED_COUNT, outs):
            if first <= v < first + count:
                for z in range(NZC):
                    lanes = pl.multiple_of(512 * z + 128 * lax.rem(y + s, 4), 128)
                    g[z, v - first] = lines[v, :, pl.ds(lanes, 128)]


def pick(inv_zeta):
    return pl.pallas_call(
        pick_kernel,
        in_specs=[HBM],
        out_specs=[VMEM] * 4,
        out_shape=[shape(NZC, count, 64, 128) for count in PICKED_COUNT],
        scratch_shapes=[pltpu.VMEM((5, 64, 4096), F32), pltpu.SemaphoreType.DMA((5,))],
        compiler_params=pltpu.CompilerParams(vmem_limit_bytes=56 << 20),
        name="pick",
    )(inv_zeta)


def prepare_kernel(*refs):
    _, eta, _, _ = position()
    own_parts, other_parts, (high2, low2, high, low, lines) = refs[:4], refs[4:8], refs[8:]
    v = pl.program_id(0)

    def place(index, own, other):
        for half, part in ((eta, own), (1 - eta, other)):
            rows = pl.ds(pl.multiple_of(64 * half, 64), 64)
            for z in range(NZC):
                lines[PICKED_STEP[index] - 1, rows, 128 * z : 128 * (z + 1)] = part[z, 0]

    for index, (own, other) in enumerate(zip(own_parts, other_parts)):
        first, count = PICKED_FIRST[index], PICKED_COUNT[index]
        if count == 5:
            place(index, own, other)
        else:
            held = jnp.logical_and(v >= first, v < first + count)
            pl.when(held)(functools.partial(place, index, own, other))
    for z in range(NZC):
        rows = slice(128 * z, 128 * (z + 1))
        high2[0, rows], low2[0, rows] = split(lines[1, :, rows].T)
        for c in range(2):
            lanes = slice(128 * c, 128 * (c + 1))
            high[0, rows, lanes], low[0, rows, lanes] = split(lines[2 * c, :, rows].T)


def prepare(own_parts, other_parts):
    widths = (128, 128, 256, 256)

    def part(first, count):
        return pl.BlockSpec(
            (NZC, 1, 64, 128), lambda v: (0, jnp.clip(v - first, 0, count - 1), 0, 0)
        )

    parts = [part(*pair) for pair in zip(PICKED_FIRST, PICKED_COUNT)]
    return pl.pallas_call(
        prepare_kernel,
        grid=(5,),
        in_specs=parts * 2,
        out_specs=[pl.BlockSpec((1, 1024, w), lambda v: (v, 0, 0)) for w in widths],
        out_shape=[shape(5, 1024, w, dtype=BF16) for w in widths],
        scratch_shapes=[pltpu.VMEM((3, 128, 1024), F32)],
        compiler_params=pltpu.CompilerParams(vmem_limit_bytes=24 << 20),
        name="prepare",
    )(*own_parts, *other_parts)


def zeta_kernel(gathered, high_hbm, low_hbm, *refs):
    *outs, field, high, low, sems = refs
    copies = []
    for v in range(5):
        pairs = (
            (gathered.at[:, v], field.at[:, v]),
            (high_hbm.at[v], high.at[v]),
            (low_hbm.at[v], low.at[v]),
        )
        copies.append([
            pltpu.make_async_copy(*pair, sems.at[v, n]) for n, pair in enumerate(pairs)
        ])
        for copy in copies[-1]:
            copy.start()
    for v in range(5):
        for copy in copies[v]:
            copy.wait()
        lines = [field[z, v].reshape(256, 128) for z in range(NZC)]
        value = dot3(split(jnp.concatenate(lines, axis=1)), (high[v], low[v]))
        for n, out in enumerate(outs):
            half, place = n % 2, n // 2
            out[v] = value[128 * half : 128 * (half + 1), 128 * place : 128 * (place + 1)]


def zeta_step(gathered, high, low):
    count = 2 * (high.shape[2] // 128)
    return pl.pallas_call(
        zeta_kernel,
        in_specs=[HBM] * 3,
        out_specs=[VMEM] * count,
        out_shape=[shape(5, 128, 128)] * count,
        scratch_shapes=[
            pltpu.VMEM(gathered.shape, F32),
            pltpu.VMEM(high.shape, BF16),
            pltpu.VMEM(low.shape, BF16),
            pltpu.SemaphoreType.DMA((5, 3)),
        ],
        compiler_params=pltpu.CompilerParams(vmem_limit_bytes=56 << 20),
        name="zeta_lines",
    )(gathered, high, low)


def own_kernel(b_ref, inv, out0, out1):
    _, _, _, y = position()
    b = split(jnp.concatenate([b_ref[z, 0].reshape(256, 128) for z in range(NZC)], axis=1))
    lanes = [pl.multiple_of(512 * z + 128 * y, 128) for z in range(NZC)]
    lines = jnp.concatenate([inv[0, :, pl.ds(lane, 128)] for lane in lanes], axis=1)
    value = dot3(b, split(lines), ((1,), (1,)))
    out0[0] = value[:128]
    out1[0] = value[128:]


def own_step(gathered, inv_zeta):
    return pl.pallas_call(
        own_kernel,
        grid=(5,),
        in_specs=[
            pl.BlockSpec((NZC, 1, 8, 32, 128), lambda v: (0, v, 0, 0, 0)),
            pl.BlockSpec((1, 128, 4096), lambda v: (v, 0, 0)),
        ],
        out_specs=[pl.BlockSpec((1, 128, 128), lambda v: (v, 0, 0))] * 2,
        out_shape=[shape(5, 128, 128)] * 2,
        compiler_params=pltpu.CompilerParams(vmem_limit_bytes=24 << 20),
        name="own_lines",
    )(gathered, inv_zeta)


def final_kernel(t_ref, state, own0, own1, low0, low1, high0, high1, out):
    for half, parts in enumerate(((own0, low0, high0), (own1, low1, high1))):

        def body(x, carry):
            rows = pl.ds(pl.multiple_of(32 * x, 32), 32)
            fields = [sum(part[v, rows] for part in parts) for v in range(5)]
            for v, value in enumerate(mixed(t_ref, 3, fields)):
                out[v, 4 * half + x] = state[v, 4 * half + x] + value
            return carry

        lax.fori_loop(0, 4, body, 0)


def final_step(transforms, state, parts):
    return pl.pallas_call(
        final_kernel,
        in_specs=[SMEM] + [VMEM] * 7,
        out_specs=VMEM,
        out_shape=shape(5, 8, 32, 128),
        compiler_params=pltpu.CompilerParams(vmem_limit_bytes=16 << 20),
        name="final",
    )(transforms, state, *parts)


def over_x(array, s):
    return lax.ppermute(array, "xi", [(i, (i + s) % 4) for i in range(4)])


def over_y(array, s):
    pairs = [(4 * z + y, 4 * z + (y + s) % 4) for z in range(NZC) for y in range(NYC)]
    return lax.ppermute(array, "zeta", pairs)


def over_core(array):
    return lax.ppermute(array, "eta", [(0, 1), (1, 0)])


def shift_line(array, axis, s):
    size = lax.axis_size(axis)
    pairs = [(i, i + s) for i in range(size) if 0 <= i + s < size]
    return lax.ppermute(array, axis, pairs)


def after(array, *first):
    return lax.optimization_barrier((array, *first))[0]


def local(state, radius, iblank, speeds, transforms, inv_xi, inv_eta, inv_zeta):
    xlo, xhi, yface, zlo, zhi = faces(state)
    halos = [
        shift_line(xhi, "xi", 1),
        shift_line(xlo, "xi", -1),
        over_core(yface),
        shift_line(zhi, "zeta", 1),
        shift_line(zlo, "zeta", -1),
    ]
    picked = pick(inv_zeta)
    halos[0] = after(halos[0], picked[0])
    residual, m0, m1, m2, m3 = residual_step(
        speeds, transforms, state, radius, iblank, inv_xi, *halos
    )
    parts = [m0] + [over_x(m, s + 1) for s, m in enumerate((m1, m2, m3))]
    sent = [over_y(after(picked[0], m0), PICKED_STEP[0])]
    b0, b1, b2, b3 = xi_step(transforms, parts)
    own = [b0] + [over_x(b, s + 1) for s, b in enumerate((b1, b2, b3))]
    other = [over_core(p) for p in own]
    own[0] = after(own[0], *sent)
    work = eta_step(transforms, inv_eta, own, other)

    columns = [[4 * z + y for z in range(NZC)] for y in range(NYC)]
    gathered = lax.all_gather(work, "zeta", axis_index_groups=columns)
    sent += [over_y(after(picked[i], work), PICKED_STEP[i]) for i in range(1, 4)]
    swapped = [over_core(after(part, work)) for part in sent]
    high2, low2, high, low = prepare(sent, swapped)

    far0, far1 = zeta_step(gathered, high2, low2)
    far0, far1 = over_y(far0, 1), over_y(far1, -1)
    down0, down1, up0, up1 = zeta_step(gathered, high, low)
    own0, own1 = own_step(gathered, after(inv_zeta, down0, up1))
    up1, down0 = over_y(up1, 1), over_y(down0, -1)
    up0, down1 = over_y(up0 + far0, 1), over_y(down1 + far1, -1)
    advanced = final_step(transforms, state, (own0, own1, up0, up1, down0, down1))
    return residual, advanced


def solution(mesh):
    placed = (
        P(None, "xi", "eta", "zeta"),
        P("xi", "eta", "zeta"),
        P("xi", "eta", "zeta"),
        P(),
        P(),
        P(None, "xi", None),
        P(None, "eta", None),
        P(None, "zeta", None),
    )
    return jax.shard_map(
        local,
        mesh=mesh,
        in_specs=placed,
        out_specs=(P(None, "xi", "eta", "zeta"), P(None, "xi", "eta", "zeta")),
        check_vma=False,
    )
```

```python
import functools

import jax
import jax.numpy as jnp
from jax import lax
from jax.experimental import pallas as pl
from jax.experimental.pallas import tpu as pltpu
from jax.sharding import PartitionSpec as P

F32 = jnp.float32
BF16 = jnp.bfloat16
SMEM = pl.BlockSpec(memory_space=pltpu.SMEM)
HBM = pl.BlockSpec(memory_space=pltpu.HBM)
VMEM = pl.BlockSpec()
NZC, NYC = 8, 4
SHIFTS = (0, 2, 1, 3)
PICKED_STEP = (2, 2, 1, 3)
PICKED_FIRST = (0, 3, 0, 0)
PICKED_COUNT = (3, 2, 5, 5)


def position():
    xi, eta, zeta = (lax.axis_index(name) for name in ("xi", "eta", "zeta"))
    return xi, eta, lax.div(zeta, 4), lax.rem(zeta, 4)


def shape(*dims, dtype=F32):
    return jax.ShapeDtypeStruct(dims, dtype)


def split(x):
    high = x.astype(BF16)
    low = (x - high.astype(F32)).astype(BF16)
    return high, low


def dot(a, b, dims):
    return lax.dot_general(a, b, (dims, ((), ())), preferred_element_type=F32)


def dot3(a, b, dims=((1,), (0,))):
    a_high, a_low = a
    b_high, b_low = b
    return dot(a_high, b_high, dims) + dot(a_high, b_low, dims) + dot(a_low, b_high, dims)


def mixed(t_ref, which, fields):
    out = []
    for a in range(5):
        total = t_ref[which, a, 0] * fields[0]
        for b in range(1, 5):
            total = total + t_ref[which, a, b] * fields[b]
        out.append(total)
    return out


def faces_kernel(state, xlo, xhi, yface, zlo, zhi):
    _, eta, _, _ = position()
    xlo[...] = state[:, 0:2]
    xhi[...] = state[:, 6:8]
    start = pl.multiple_of(24 * (1 - eta), 8)
    yface[...] = state[:, :, pl.ds(start, 8), :]
    for c in range(10):
        v, x = divmod(4 * c, 8)
        t = state[v, x : x + 4].reshape(128, 128).T
        zlo[:, 128 * c : 128 * (c + 1)] = t[0:8]
        zhi[:, 128 * c : 128 * (c + 1)] = t[120:128]


def faces(state):
    return pl.pallas_call(
        faces_kernel,
        in_specs=[VMEM],
        out_specs=[VMEM] * 5,
        out_shape=[
            shape(5, 2, 32, 128),
            shape(5, 2, 32, 128),
            shape(5, 8, 8, 128),
            shape(8, 1280),
            shape(8, 1280),
        ],
        name="faces",
    )(state)


def residual_kernel(
    speeds, t_ref, state, radius_hbm, iblank_hbm, inv_xi_hbm, xprev, xnext, yrec, zprev, znext,
    residual, m0, m1, m2, m3, ext, radius, iblank, inv_xi, zface, w0, sems,
):
    xi, eta, _, _ = position()
    copies = [
        pltpu.make_async_copy(state, ext.at[:, pl.ds(2, 8)], sems.at[0]),
        pltpu.make_async_copy(radius_hbm, radius, sems.at[1]),
        pltpu.make_async_copy(iblank_hbm, iblank, sems.at[2]),
        pltpu.make_async_copy(inv_xi_hbm, inv_xi, sems.at[3]),
    ]
    for copy in copies:
        copy.start()
    ext[:, 0:2] = xprev[...]
    ext[:, 10:12] = xnext[...]
    for c in range(10):
        v, x = divmod(4 * c, 8)
        lanes = slice(128 * c, 128 * (c + 1))
        t = jnp.concatenate([znext[:, lanes], jnp.zeros((112, 128), F32), zprev[:, lanes]], axis=0)
        zface[v, x : x + 4] = t.T.reshape(4, 32, 128)
    lane = lax.broadcasted_iota(jnp.int32, (32, 128), 1)
    row = lax.broadcasted_iota(jnp.int32, (32, 128), 0)
    has_low = eta == 1
    for copy in copies:
        copy.wait()

    def body(x, carry):
        rad = 0.04 * radius[x]
        keep = -iblank[x].astype(F32)
        fields = []
        for v in range(5):
            q = ext[v, x + 2]
            xp, xm = ext[v, x + 3], ext[v, x + 1]
            xpp, xmm = ext[v, x + 4], ext[v, x]
            face = yrec[v, x]
            lows = jnp.where(has_low, face, 0.0)
            highs = jnp.where(has_low, 0.0, face)
            l2, l1 = lows[6:7], lows[7:8]
            h1, h2 = highs[0:1], highs[1:2]
            yp = jnp.where(row == 31, h1, pltpu.roll(q, 31, 0))
            ypp = jnp.where(row == 31, h2, jnp.where(row == 30, h1, pltpu.roll(q, 30, 0)))
            ym = jnp.where(row == 0, l1, pltpu.roll(q, 1, 0))
            ymm = jnp.where(row == 0, l2, jnp.where(row == 1, l1, pltpu.roll(q, 2, 0)))
            z = zface[v, x]
            zp = pltpu.roll(jnp.where(lane == 0, z, q), 127, 1)
            zpp = pltpu.roll(jnp.where(lane < 2, z, q), 126, 1)
            zm = pltpu.roll(jnp.where(lane == 127, z, q), 1, 1)
            zmm = pltpu.roll(jnp.where(lane >= 126, z, q), 2, 1)
            flux = (
                (0.5 * speeds[0, v]) * (xp - xm)
                + (0.5 * speeds[1, v]) * (yp - ym)
                + (0.5 * speeds[2, v]) * (zp - zm)
            )
            far = (xpp + xmm) + (ypp + ymm) + (zpp + zmm)
            near = (xp + xm) + (yp + ym) + (zp + zm)
            diss = rad * (far - 4.0 * near + 18.0 * q)
            r = keep * (flux + diss)
            residual[v, x] = r
            fields.append(r)
        for v, value in enumerate(mixed(t_ref, 0, fields)):
            w0[v, x] = value
        return carry

    lax.fori_loop(0, 8, body, 0)
    for s, m in zip(SHIFTS, (m0, m1, m2, m3)):
        start = pl.multiple_of(8 * lax.rem(xi + s, 4), 8)
        m[:, 0:8] = w0[:, :, pl.ds(start, 8), :]
        m[:, 8] = jnp.concatenate([inv_xi[...], jnp.zeros((5, 8, 96), F32)], axis=2)


def residual_step(speeds, transforms, *arrays):
    return pl.pallas_call(
        residual_kernel,
        in_specs=[SMEM] * 2 + [HBM] * 4 + [VMEM] * 5,
        out_specs=[VMEM] * 5,
        out_shape=[shape(5, 8, 32, 128)] + [shape(5, 9, 8, 128)] * 4,
        scratch_shapes=[
            pltpu.VMEM((5, 12, 32, 128), F32),
            pltpu.VMEM((8, 32, 128), F32),
            pltpu.VMEM((8, 32, 128), jnp.int32),
            pltpu.VMEM((5, 8, 32), F32),
            pltpu.VMEM((5, 8, 32, 128), F32),
            pltpu.VMEM((5, 8, 32, 128), F32),
            pltpu.SemaphoreType.DMA((4,)),
        ],
        compiler_params=pltpu.CompilerParams(vmem_limit_bytes=16 << 20),
        name="residual",
    )(speeds, transforms, *arrays)


def xi_kernel(t_ref, r0, r1, r2, r3, b0, b1, b2, b3, field, inverse, work):
    xi, _, _, _ = position()
    for s, r in zip(SHIFTS, (r0, r1, r2, r3)):
        start = pl.multiple_of(8 * lax.rem(xi + 4 - s, 4), 8)
        field[:, pl.ds(start, 8)] = r[:, 0:8]
        inverse[:, pl.ds(start, 8), :] = r[:, 8]
    rows = lax.broadcasted_iota(jnp.int32, (256, 32), 0) // 8
    spread = (rows == lax.broadcasted_iota(jnp.int32, (256, 32), 1)).astype(F32).astype(BF16)
    cols = lax.broadcasted_iota(jnp.int32, (128, 256), 1) // 8
    widen = (cols == lax.broadcasted_iota(jnp.int32, (128, 256), 0)).astype(F32).astype(BF16)
    same = (
        lax.broadcasted_iota(jnp.int32, (256, 256), 0) % 8
        == lax.broadcasted_iota(jnp.int32, (256, 256), 1) % 8
    )
    for v in range(5):
        line = []
        for part in split(inverse[v]):
            wide = dot(part, widen, ((1,), (0,))).astype(BF16)
            full = dot(spread, wide, ((1,), (0,)))
            line.append(jnp.where(same, full, 0.0).astype(BF16))
        value = dot3(line, split(field[v].reshape(256, 128)))
        work[v] = value.reshape(32, 8, 128)

    def body(x, carry):
        for v, value in enumerate(mixed(t_ref, 1, [work[v, x] for v in range(5)])):
            field[v, x] = value
        return carry

    lax.fori_loop(0, 32, body, 0)
    for s, b in zip(SHIFTS, (b0, b1, b2, b3)):
        b[...] = field[:, pl.ds(8 * lax.rem(xi + s, 4), 8)]


def xi_step(transforms, parts):
    return pl.pallas_call(
        xi_kernel,
        in_specs=[SMEM] + [VMEM] * 4,
        out_specs=[VMEM] * 4,
        out_shape=[shape(5, 8, 8, 128)] * 4,
        scratch_shapes=[
            pltpu.VMEM((5, 32, 8, 128), F32),
            pltpu.VMEM((5, 32, 128), F32),
            pltpu.VMEM((5, 32, 8, 128), F32),
        ],
        compiler_params=pltpu.CompilerParams(vmem_limit_bytes=16 << 20),
        name="xi_lines",
    )(transforms, *parts)


def eta_kernel(t_ref, inv_eta, p0, p1, p2, p3, q0, q1, q2, q3, out, field, work):
    xi, eta, _, _ = position()
    for s, p, q in zip(SHIFTS, (p0, p1, p2, p3), (q0, q1, q2, q3)):
        rows = 8 * lax.rem(xi + 4 - s, 4)
        field[:, :, pl.ds(pl.multiple_of(32 * eta + rows, 8), 8), :] = p[...]
        field[:, :, pl.ds(pl.multiple_of(32 * (1 - eta) + rows, 8), 8), :] = q[...]
    for v in range(5):
        wide = jnp.concatenate([field[v, x] for x in range(8)], axis=1)
        value = dot3(split(inv_eta[v]), split(wide))
        for x in range(8):
            work[v, x] = value[:, 128 * x : 128 * (x + 1)]


    def body(x, carry):
        for v, value in enumerate(mixed(t_ref, 2, [work[v, x] for v in range(5)])):
            out[v, x] = value
        return carry

    lax.fori_loop(0, 8, body, 0)


def eta_step(transforms, inv_eta, own, other):
    return pl.pallas_call(
        eta_kernel,
        in_specs=[SMEM] + [VMEM] * 9,
        out_specs=VMEM,
        out_shape=shape(5, 8, 32, 128),
        scratch_shapes=[pltpu.VMEM((5, 8, 64, 128), F32), pltpu.VMEM((5, 8, 32, 128), F32)],
        compiler_params=pltpu.CompilerParams(vmem_limit_bytes=16 << 20),
        name="eta_lines",
    )(transforms, inv_eta, *own, *other)


def pick_kernel(inv, *refs):
    _, eta, _, y = position()
    *outs, lines, sems = refs
    rows = pl.ds(pl.multiple_of(64 * eta, 64), 64)
    copies = [
        pltpu.make_async_copy(inv.at[v, rows], lines.at[v], sems.at[v]) for v in range(5)
    ]
    for copy in copies:
        copy.start()
    for v, copy in enumerate(copies):
        copy.wait()
        for s, first, count, g in zip(PICKED_STEP, PICKED_FIRST, PICKED_COUNT, outs):
            if first <= v < first + count:
                for z in range(NZC):
                    lanes = pl.multiple_of(512 * z + 128 * lax.rem(y + s, 4), 128)
                    g[z, v - first] = lines[v, :, pl.ds(lanes, 128)]


def pick(inv_zeta):
    return pl.pallas_call(
        pick_kernel,
        in_specs=[HBM],
        out_specs=[VMEM] * 4,
        out_shape=[shape(NZC, count, 64, 128) for count in PICKED_COUNT],
        scratch_shapes=[pltpu.VMEM((5, 64, 4096), F32), pltpu.SemaphoreType.DMA((5,))],
        compiler_params=pltpu.CompilerParams(vmem_limit_bytes=56 << 20),
        name="pick",
    )(inv_zeta)


def prepare_kernel(*refs):
    _, eta, _, _ = position()
    own_parts, other_parts, (high2, low2, high, low, lines) = refs[:4], refs[4:8], refs[8:]
    v = pl.program_id(0)

    def place(index, own, other):
        for half, part in ((eta, own), (1 - eta, other)):
            rows = pl.ds(pl.multiple_of(64 * half, 64), 64)
            for z in range(NZC):
                lines[PICKED_STEP[index] - 1, rows, 128 * z : 128 * (z + 1)] = part[z, 0]

    for index, (own, other) in enumerate(zip(own_parts, other_parts)):
        first, count = PICKED_FIRST[index], PICKED_COUNT[index]
        if count == 5:
            place(index, own, other)
        else:
            held = jnp.logical_and(v >= first, v < first + count)
            pl.when(held)(functools.partial(place, index, own, other))
    for z in range(NZC):
        rows = slice(128 * z, 128 * (z + 1))
        high2[0, rows], low2[0, rows] = split(lines[1, :, rows].T)
        for c in range(2):
            lanes = slice(128 * c, 128 * (c + 1))
            high[0, rows, lanes], low[0, rows, lanes] = split(lines[2 * c, :, rows].T)


def prepare(own_parts, other_parts):
    widths = (128, 128, 256, 256)

    def part(first, count):
        return pl.BlockSpec(
            (NZC, 1, 64, 128), lambda v: (0, jnp.clip(v - first, 0, count - 1), 0, 0)
        )

    parts = [part(*pair) for pair in zip(PICKED_FIRST, PICKED_COUNT)]
    return pl.pallas_call(
        prepare_kernel,
        grid=(5,),
        in_specs=parts * 2,
        out_specs=[pl.BlockSpec((1, 1024, w), lambda v: (v, 0, 0)) for w in widths],
        out_shape=[shape(5, 1024, w, dtype=BF16) for w in widths],
        scratch_shapes=[pltpu.VMEM((3, 128, 1024), F32)],
        compiler_params=pltpu.CompilerParams(vmem_limit_bytes=24 << 20),
        name="prepare",
    )(*own_parts, *other_parts)


def zeta_kernel(gathered, high_hbm, low_hbm, *refs):
    *outs, field, high, low, sems = refs
    copies = []
    for v in range(5):
        pairs = (
            (gathered.at[:, v], field.at[:, v]),
            (high_hbm.at[v], high.at[v]),
            (low_hbm.at[v], low.at[v]),
        )
        copies.append([
            pltpu.make_async_copy(*pair, sems.at[v, n]) for n, pair in enumerate(pairs)
        ])
        for copy in copies[-1]:
            copy.start()
    for v in range(5):
        for copy in copies[v]:
            copy.wait()
        lines = [field[z, v].reshape(256, 128) for z in range(NZC)]
        value = dot3(split(jnp.concatenate(lines, axis=1)), (high[v], low[v]))
        for n, out in enumerate(outs):
            half, place = n % 2, n // 2
            out[v] = value[128 * half : 128 * (half + 1), 128 * place : 128 * (place + 1)]


def zeta_step(gathered, high, low):
    count = 2 * (high.shape[2] // 128)
    return pl.pallas_call(
        zeta_kernel,
        in_specs=[HBM] * 3,
        out_specs=[VMEM] * count,
        out_shape=[shape(5, 128, 128)] * count,
        scratch_shapes=[
            pltpu.VMEM(gathered.shape, F32),
            pltpu.VMEM(high.shape, BF16),
            pltpu.VMEM(low.shape, BF16),
            pltpu.SemaphoreType.DMA((5, 3)),
        ],
        compiler_params=pltpu.CompilerParams(vmem_limit_bytes=56 << 20),
        name="zeta_lines",
    )(gathered, high, low)


def own_kernel(b_ref, inv, out0, out1):
    _, _, _, y = position()
    b = split(jnp.concatenate([b_ref[z, 0].reshape(256, 128) for z in range(NZC)], axis=1))
    lanes = [pl.multiple_of(512 * z + 128 * y, 128) for z in range(NZC)]
    lines = jnp.concatenate([inv[0, :, pl.ds(lane, 128)] for lane in lanes], axis=1)
    value = dot3(b, split(lines), ((1,), (1,)))
    out0[0] = value[:128]
    out1[0] = value[128:]


def own_step(gathered, inv_zeta):
    return pl.pallas_call(
        own_kernel,
        grid=(5,),
        in_specs=[
            pl.BlockSpec((NZC, 1, 8, 32, 128), lambda v: (0, v, 0, 0, 0)),
            pl.BlockSpec((1, 128, 4096), lambda v: (v, 0, 0)),
        ],
        out_specs=[pl.BlockSpec((1, 128, 128), lambda v: (v, 0, 0))] * 2,
        out_shape=[shape(5, 128, 128)] * 2,
        compiler_params=pltpu.CompilerParams(vmem_limit_bytes=24 << 20),
        name="own_lines",
    )(gathered, inv_zeta)


def final_kernel(t_ref, state, own0, own1, low0, low1, high0, high1, out):
    for half, parts in enumerate(((own0, low0, high0), (own1, low1, high1))):

        def body(x, carry):
            rows = pl.ds(pl.multiple_of(32 * x, 32), 32)
            fields = [sum(part[v, rows] for part in parts) for v in range(5)]
            for v, value in enumerate(mixed(t_ref, 3, fields)):
                out[v, 4 * half + x] = state[v, 4 * half + x] + value
            return carry

        lax.fori_loop(0, 4, body, 0)


def final_step(transforms, state, parts):
    return pl.pallas_call(
        final_kernel,
        in_specs=[SMEM] + [VMEM] * 7,
        out_specs=VMEM,
        out_shape=shape(5, 8, 32, 128),
        compiler_params=pltpu.CompilerParams(vmem_limit_bytes=16 << 20),
        name="final",
    )(transforms, state, *parts)


def over_x(array, s):
    return lax.ppermute(array, "xi", [(i, (i + s) % 4) for i in range(4)])


def over_y(array, s):
    pairs = [(4 * z + y, 4 * z + (y + s) % 4) for z in range(NZC) for y in range(NYC)]
    return lax.ppermute(array, "zeta", pairs)


def over_core(array):
    return lax.ppermute(array, "eta", [(0, 1), (1, 0)])


def shift_line(array, axis, s):
    size = lax.axis_size(axis)
    pairs = [(i, i + s) for i in range(size) if 0 <= i + s < size]
    return lax.ppermute(array, axis, pairs)


def after(array, *first):
    return lax.optimization_barrier((array, *first))[0]


def local(state, radius, iblank, speeds, transforms, inv_xi, inv_eta, inv_zeta):
    xlo, xhi, yface, zlo, zhi = faces(state)
    halos = [
        shift_line(xhi, "xi", 1),
        shift_line(xlo, "xi", -1),
        over_core(yface),
        shift_line(zhi, "zeta", 1),
        shift_line(zlo, "zeta", -1),
    ]
    picked = pick(inv_zeta)
    halos[0] = after(halos[0], picked[0])
    residual, m0, m2, m1, m3 = residual_step(
        speeds, transforms, state, radius, iblank, inv_xi, *halos
    )
    r2, r1, r3 = over_x(m2, 2), over_x(m1, 1), over_x(m3, 3)
    parts = [m0, r2, r1, r3]
    sent = [over_y(after(picked[0], m0), PICKED_STEP[0])]
    b0, b2, b1, b3 = xi_step(transforms, parts)
    p2, p1, p3 = over_x(b2, 2), over_x(b1, 1), over_x(b3, 3)
    own = [b0, p2, p1, p3]
    other = [over_core(p) for p in own]
    own[0] = after(own[0], *sent)
    work = eta_step(transforms, inv_eta, own, other)

    columns = [[4 * z + y for z in range(NZC)] for y in range(NYC)]
    gathered = lax.all_gather(work, "zeta", axis_index_groups=columns)
    sent += [over_y(after(picked[i], work), PICKED_STEP[i]) for i in range(1, 4)]
    swapped = [over_core(after(part, work)) for part in sent]
    high2, low2, high, low = prepare(sent, swapped)

    far0, far1 = zeta_step(gathered, high2, low2)
    far0, far1 = over_y(far0, 1), over_y(far1, -1)
    down0, down1, up0, up1 = zeta_step(gathered, high, low)
    own0, own1 = own_step(gathered, after(inv_zeta, down0, up1))
    up1, down0 = over_y(up1, 1), over_y(down0, -1)
    up0, down1 = over_y(up0 + far0, 1), over_y(down1 + far1, -1)
    advanced = final_step(transforms, state, (own0, own1, up0, up1, down0, down1))
    return residual, advanced


def solution(mesh):
    placed = (
        P(None, "xi", "eta", "zeta"),
        P("xi", "eta", "zeta"),
        P("xi", "eta", "zeta"),
        P(),
        P(),
        P(None, "xi", None),
        P(None, "eta", None),
        P(None, "zeta", None),
    )
    return jax.shard_map(
        local,
        mesh=mesh,
        in_specs=placed,
        out_specs=(P(None, "xi", "eta", "zeta"), P(None, "xi", "eta", "zeta")),
        check_vma=False,
    )
```
